128 devices in a mesh: exp: 16 (over y, z_lo, core), fsdp: 8 (over z_hi, x).
Axes of the slice: x: 4, y: 4, z: 4 (z_hi: 2, z_lo: 2; z = z_hi * 2 + z_lo), core: 2. Of those that a mesh axis runs over, the one named last changes fastest.
Arguments:
- tokens: bfloat16 [16384, 2048], P(('exp', 'fsdp')), may hold values from -6 to 6
- cotangent: bfloat16 [16384, 2048], P(('exp', 'fsdp')), may hold values from -0.29882812 to 0.29882812
- routes: int32 [16384, 6], P(('exp', 'fsdp')), may hold values from 0 to 31, all different within a row; in each aligned block of 128 rows (0 to 127, 128 to 255, ...) at most 28 rows name the same one
- probs: float32 [16384, 6], P(('exp', 'fsdp')), may hold values from 0.1 to 1
- w_gate_up: bfloat16 [32, 2048, 1408], P('exp', 'fsdp'), may hold values from -0.125 to 0.125
- w_down: bfloat16 [32, 704, 2048], P('exp', None, 'fsdp'), may hold values from -0.21875 to 0.21875
Outputs:
- d_tokens: bfloat16 [16384, 2048], P(('exp', 'fsdp'))
- d_probs: float32 [16384, 6], P(('exp', 'fsdp'))
- grad_gate_up: bfloat16 [32, 2048, 1408], P('exp', 'fsdp')
- grad_down: bfloat16 [32, 704, 2048], P('exp', None, 'fsdp')
The draws below stay inside these ranges and needn't reach their ends.
Inputs may be any that keep to these rules, and one draw needn't show every extreme that they name: `routes`: each row names 6 different experts; among the rows of one device no expert is named more than 28 times.
All inputs are finite; a program needn't handle non-finite values.
Results may differ from the reference program's by a relative error of at most 0.02.
Values may be sent and summed in bfloat16 or wider, within the bound.
No kernel may reach another device: no remote copies, remote signals or barrier semaphores. Data moves between devices by JAX's collectives and lax.ppermute only.
A program may use at most 128 MiB of HBM per device.

```python
import math
import jax
import jax.numpy as jnp
import numpy as np
from jax import lax

D = 2048
F = 704
TOP = 6
TOK_DEV = 128
EXPERTS = 32
CAP = 28
TOKENS = 16384
N_EXP = 16
N_FSDP = 8


def level_of(rng, dims, pieces, smallest, top_value):
    gain = 1.0
    for position, shards_of in pieces:
        steps = jax.random.uniform(jax.random.fold_in(jax.random.fold_in(rng, 6), position), (shards_of,), jnp.float32, smallest / len(pieces), top_value / len(pieces))
        gain = gain * jnp.repeat(jnp.exp(steps), dims[position] // shards_of).reshape((-1,) + (1,) * (len(dims) - 1 - position))
    return gain


def shared_out(stream_key, own, number, rows, count, top, limit, lean):
    sequence = jax.random.permutation(stream_key, count)
    crowded, ordinary = shares(count, rows * top, limit, lean, True), shares(count, rows * top, limit, lean, False)
    places = jnp.arange(count)

    def named(tallies, rotation):
        used = int((tallies > 0).sum())
        fixed = max(1, used // 4)
        moved = fixed + (places - fixed + rotation * (used - fixed)) % max(1, count - fixed)
        return jnp.zeros((count,), jnp.int32).at[sequence[jnp.where(places < fixed, places, moved)]].set(jnp.asarray(tallies, jnp.int32))

    tallies = jnp.where(number % 4 == 0, named(crowded, number // 4), named(ordinary, number - number // 4 - 1))
    mixed = jax.random.permutation(jax.random.fold_in(own, 3), count)
    donor, receiver = mixed[0:count // 2 * 2:2], mixed[1:count // 2 * 2:2]
    margin = jnp.minimum(tallies[donor] - 1, limit - tallies[receiver]) // 2
    margin = jnp.where((donor == sequence[0]) | (receiver == sequence[0]) | (tallies[receiver] == 0), 0, jnp.maximum(margin, 0))
    moved = jax.random.randint(jax.random.fold_in(own, 4), (count // 2,), 0, 1 << 20) % (margin + 1)
    tallies = tallies.at[donor].add(-moved).at[receiver].add(moved)
    labels = jnp.searchsorted(jnp.cumsum(tallies), jnp.arange(rows * top), side="right").astype(jnp.int32)
    table = labels.reshape(top, rows).T
    table = table[jax.random.permutation(jax.random.fold_in(own, 1), rows)]
    rotation = jax.random.randint(jax.random.fold_in(own, 2), (rows, 1), 0, top)
    return jnp.take_along_axis(table, (jnp.arange(top)[None, :] + rotation) % top, axis=1)


def shares(amount, total, limit, slope, full):
    portions = [(1 << 20) // math.isqrt(rank ** slope) + 1 for rank in range(1, amount + 1)]
    largest = limit if full else min(limit, max(-(-total // amount), total * portions[0] // sum(portions)))
    least = 1 if total - largest >= amount - 1 else 0
    counts, rest = [largest] + [least] * (amount - 1), total - largest - least * (amount - 1)
    while rest > 0:
        movable = [i for i in range(1, amount) if counts[i] < largest] or [i for i in range(1, amount) if counts[i] < limit]
        pool, budget = sum([portions[i] for i in movable]), rest
        for i in movable:
            more = min(limit - counts[i], max(1, budget * portions[i] // pool), rest)
            counts[i] = counts[i] + more
            rest = rest - more
    return np.array(counts)


def scatter_about(key, extent, deviation, limit, cuts=(), held_as=jnp.bfloat16):
    drawn = deviation * jax.random.normal(key, extent, jnp.float32)
    if cuts:
        drawn = drawn * level_of(key, extent, cuts, -0.22, 0.18)
    return jnp.clip(drawn, -limit, limit).astype(held_as)


def setup_inputs(seed: int = 0) -> dict:
    arg_keys = jax.random.split(jax.random.key(seed), 7)
    tokens = scatter_about(arg_keys[0], (TOKENS, D), 1.0, 6.0, ((0, 128),))
    cotangent = scatter_about(arg_keys[1], (TOKENS, D), 0.05, 0.29882812, ((0, 128),))
    routes_keys = jax.random.split(jax.random.fold_in(arg_keys[2], 1), TOKENS // TOK_DEV)
    routes_turns = jax.random.permutation(jax.random.fold_in(arg_keys[2], 3), TOKENS // TOK_DEV)
    routes = jax.vmap(lambda own, number: shared_out(jax.random.fold_in(arg_keys[2], 2), own, number, TOK_DEV, EXPERTS, TOP, CAP, 1))(routes_keys, routes_turns).reshape((TOKENS, TOP))
    probs = jnp.clip(0.1 + 0.9 * jax.random.uniform(arg_keys[3], (TOKENS, TOP), jnp.float32) ** level_of(arg_keys[3], (TOKENS, TOP), ((0, 128),), -0.2, 0.2), 0.1, 1.0)
    w_gate_up = scatter_about(arg_keys[4], (EXPERTS, D, 2 * F), D ** -0.5, 0.125, ((0, 16), (1, 8)))
    w_down = scatter_about(arg_keys[5], (EXPERTS, F, D), F ** -0.5, 0.21875, ((0, 16), (2, 8)))
    return dict(tokens=tokens, cotangent=cotangent, routes=routes, probs=probs, w_gate_up=w_gate_up, w_down=w_down)


def expert_rows(rows_in, cotan_rows, weights_in, gate_up_matrix, down_matrix):
    half = gate_up_matrix.shape[1] // 2
    both = jnp.dot(rows_in, gate_up_matrix, preferred_element_type=jnp.float32)
    gate_value = both[:, :half]
    up_value = both[:, half:]
    logistic = jax.nn.sigmoid(gate_value)
    activated = gate_value * logistic
    hidden = (activated * up_value).astype(jnp.bfloat16)
    expert_out = jnp.dot(hidden, down_matrix, preferred_element_type=jnp.float32)
    prob_grad = jnp.sum(cotan_rows.astype(jnp.float32) * expert_out, axis=1)
    scaled = (weights_in[:, None] * cotan_rows.astype(jnp.float32)).astype(jnp.bfloat16)
    back_proj = lax.dot_general(cotan_rows, down_matrix, (((1,), (1,)), ((), ())), preferred_element_type=jnp.float32)
    d_hidden = weights_in[:, None] * back_proj
    d_upper = (d_hidden * activated).astype(jnp.bfloat16)
    d_gating = (d_hidden * up_value * logistic * (1.0 + gate_value * (1.0 - logistic))).astype(jnp.bfloat16)
    d_both = jnp.concatenate([d_gating, d_upper], axis=1)
    part_gate_up = lax.dot_general(rows_in, d_both, (((0,), (0,)), ((), ())), preferred_element_type=jnp.float32)
    part_down = lax.dot_general(hidden, scaled, (((0,), (0,)), ((), ())), preferred_element_type=jnp.float32)
    copy_grad = lax.dot_general(d_both, gate_up_matrix, (((1,), (1,)), ((), ())), preferred_element_type=jnp.float32)
    return part_gate_up, part_down, copy_grad.astype(jnp.bfloat16), prob_grad


def round_trip(value):
    return lax.optimization_barrier(value.astype(jnp.bfloat16)).astype(jnp.float32)


def reference(tokens, cotangent, routes, probs, w_gate_up, w_down):
    copies = TOKENS * TOP
    row_limit = N_EXP * CAP
    flat_routes = routes.reshape(-1).astype(jnp.int32)
    flat_probs = probs.reshape(-1)
    positions = jnp.arange(copies, dtype=jnp.int32)
    fsdp_group = (positions // (TOP * TOK_DEV)) % N_FSDP

    def per_expert(carry, expert):
        def per_group(inner, group_index):
            dx_total, dprob_total, total_gate_up, total_down = inner
            chosen = (flat_routes == expert) & (fsdp_group == group_index)
            picked = jnp.nonzero(chosen, size=row_limit, fill_value=copies)[0].astype(jnp.int32)
            present = picked < copies
            safe_index = jnp.minimum(picked, copies - 1)
            token_index = safe_index // TOP
            rows_in = tokens[token_index]
            cotan_rows = cotangent[token_index]
            weights_in = jnp.where(present, flat_probs[safe_index], jnp.zeros((), flat_probs.dtype))
            part_gate_up, part_down, copy_grad, prob_grad = expert_rows(
                rows_in, cotan_rows, weights_in, w_gate_up[expert], w_down[expert])
            landing = jnp.where(present, token_index, TOKENS).astype(jnp.int32)
            dx_total = dx_total.at[landing].add(copy_grad.astype(jnp.float32), mode="drop")
            dprob_total = dprob_total.at[picked].set(prob_grad, mode="drop")
            total_gate_up = total_gate_up + round_trip(part_gate_up)
            total_down = total_down + round_trip(part_down)
            return (dx_total, dprob_total, total_gate_up, total_down), None

        start = (carry[0], carry[1], jnp.zeros((D, 2 * F), jnp.float32), jnp.zeros((F, D), jnp.float32))
        inner, _ = lax.scan(per_group, start, jnp.arange(N_FSDP, dtype=jnp.int32))
        dx_total, dprob_total, total_gate_up, total_down = inner
        return (dx_total, dprob_total), (total_gate_up.astype(jnp.bfloat16), total_down.astype(jnp.bfloat16))

    initial = (jnp.zeros((TOKENS, D), jnp.float32), jnp.zeros((copies,), jnp.float32))
    final, stacked = lax.scan(per_expert, initial, jnp.arange(EXPERTS, dtype=jnp.int32))
    dx_total, dprob_total = final
    grad_gate_up, grad_down = stacked
    return dx_total.astype(jnp.bfloat16), dprob_total.reshape(TOKENS, TOP), grad_gate_up, grad_down
```

```python
import jax
import jax.numpy as jnp
from jax import lax
from jax.experimental import pallas as pl
from jax.experimental.pallas import tpu as pltpu
from jax.sharding import Mesh, PartitionSpec as P

TOP = 6
CAP = 28
D = 2048
F = 704
TOK = 128
WIDE = D + 128
ROWS = 8 * 4 * CAP
BLK = 4 * CAP
BF = jnp.bfloat16
F32 = jnp.float32
MIB = 1 << 20


def params(mib=48):
    return pltpu.CompilerParams(vmem_limit_bytes=mib * MIB)


def mm(a, b, ca=1, cb=0):
    return lax.dot_general(a, b, (((ca,), (cb,)), ((), ())), preferred_element_type=F32)


def whole(shape):
    return pl.BlockSpec(shape, lambda *_: (0,) * len(shape))


def cost(flops, moved):
    return pl.CostEstimate(flops=flops, bytes_accessed=moved, transcendentals=0)


def meta_kernel(tok, cot, routes, probs, out_tok, out_cot):
    lane = lax.broadcasted_iota(jnp.int32, (TOK, 128), 1)
    meta = jnp.zeros((TOK, 128), F32)
    chosen = routes[...].astype(F32)
    weight = probs[...]
    for k in range(TOP):
        meta = jnp.where(lane == k, chosen[:, k : k + 1], meta)
        meta = jnp.where(lane == 8 + k, weight[:, k : k + 1], meta)
    meta = meta.astype(BF)
    out_tok[:, :D] = tok[...]
    out_tok[:, D:] = meta
    out_cot[:, :D] = cot[...]
    out_cot[:, D:] = meta


def add_meta(tokens, cotangent, routes, probs):
    shape = jax.ShapeDtypeStruct((TOK, WIDE), BF)
    return pl.pallas_call(
        meta_kernel,
        out_shape=(shape, shape),
        compiler_params=params(16),
        cost_estimate=cost(0, 4 * TOK * WIDE * 2),
    )(tokens, cotangent, routes, probs)


def pick_matrix(metas, experts, bases, weighted, sel):
    earlier = (
        lax.broadcasted_iota(jnp.int32, (TOK, TOK), 0)
        < lax.broadcasted_iota(jnp.int32, (TOK, TOK), 1)
    ).astype(BF)
    places, weights = [], []
    for d in range(4):
        turned = metas[d][...].astype(F32).T
        mask = jnp.zeros((8, TOK), F32)
        weight = jnp.zeros((8, TOK), F32)
        for k in range(TOP):
            hit = turned[k : k + 1, :] == experts
            mask = jnp.where(hit, 1.0, mask)
            weight = jnp.where(hit, turned[8 + k : 9 + k, :], weight)
        rank = mm(mask.astype(BF), earlier)
        places.append(jnp.where(mask > 0.5, rank + bases[d], -1.0))
        weights.append(weight if weighted else mask)
    place = jnp.concatenate(places, axis=1)
    weight = jnp.concatenate(weights, axis=1)
    row = lax.broadcasted_iota(jnp.int32, (BLK, 4 * TOK), 0).astype(F32)
    for j in range(8):
        sel[j * BLK : (j + 1) * BLK, :] = jnp.where(
            row == place[j : j + 1, :], weight[j : j + 1, :], 0.0
        ).astype(BF)


def pick_tokens_kernel(sc, t0, t1, t2, t3, m0, m1, m2, m3, out, sel):
    y = sc[0]

    @pl.when(pl.program_id(0) == 0)
    def _():
        experts = (y * 8 + lax.broadcasted_iota(jnp.int32, (8, TOK), 0)).astype(F32)
        bases = [(((y - d) & 3) * CAP).astype(F32) for d in range(4)]
        pick_matrix((m0, m1, m2, m3), experts, bases, False, sel)

    table = jnp.concatenate([t0[...], t1[...], t2[...], t3[...]], axis=0)
    out[...] = mm(sel[...], table).astype(BF)


def pick_cotan_kernel(sc, t0, t1, t2, t3, m0, m1, m2, m3, *rest):
    outs, sel = rest[:8], rest[8]
    y, z_lo, core, z_hi = sc[0], sc[1], sc[2], sc[3]
    z = z_hi * 2 + z_lo

    @pl.when(pl.program_id(0) == 0)
    def _():
        index = lax.broadcasted_iota(jnp.int32, (8, TOK), 0)
        experts = jnp.zeros((8, TOK), jnp.int32)
        for j in range(8):
            to_y, to_core = (y + j % 4) & 3, core ^ (j // 4)
            experts = jnp.where(
                index == j, ((to_y * 2 + z_lo) * 2 + to_core) * 2 + z_hi, experts
            )
        bases = [(((z - d) & 3) * CAP).astype(F32) for d in range(4)]
        pick_matrix((m0, m1, m2, m3), experts.astype(F32), bases, True, sel)

    table = jnp.concatenate([t0[...], t1[...], t2[...], t3[...]], axis=0)
    rows = mm(sel[...], table).astype(BF)
    for j in range(8):
        outs[j][...] = rows[j * BLK : (j + 1) * BLK, :]


def pick(kernel, sc, sources, split):
    step = 512
    column = lambda n, sc: (0, n)
    last = lambda n, sc: (0, D // 128)
    if split:
        out_shape = [jax.ShapeDtypeStruct((BLK, D), BF)] * 8
        out_specs = [pl.BlockSpec((BLK, step), column)] * 8
        scratch = [pltpu.VMEM((ROWS, 4 * TOK), BF)]
    else:
        out_shape = [
            jax.ShapeDtypeStruct((ROWS, D), BF),
            jax.ShapeDtypeStruct((ROWS, 4 * TOK), BF),
        ]
        out_specs = [
            pl.BlockSpec((ROWS, step), column),
            pl.BlockSpec((ROWS, 4 * TOK), lambda n, sc: (0, 0)),
        ]
        scratch = []
    return pl.pallas_call(
        kernel,
        grid_spec=pltpu.PrefetchScalarGridSpec(
            num_scalar_prefetch=1,
            grid=(D // step,),
            in_specs=[pl.BlockSpec((TOK, step), column)] * 4
            + [pl.BlockSpec((TOK, 128), last)] * 4,
            out_specs=out_specs,
            scratch_shapes=scratch,
        ),
        out_shape=out_shape,
        compiler_params=params(),
        cost_estimate=cost(2 * ROWS * 512 * D, 6 * MIB),
    )(sc, *sources, *sources)


def forward_kernel(sc, rows, w_own, w_oth, hidden, act, slope):
    z_hi = sc[3]
    own = pl.multiple_of(z_hi * 1024, 1024)
    oth = pl.multiple_of((1 - z_hi) * 1024, 1024)
    both = mm(rows[:, pl.ds(own, 1024)], w_own[...]) + mm(
        rows[:, pl.ds(oth, 1024)], w_oth[...]
    )
    gate, up = both[:, :F], both[:, F:]
    logistic = jax.nn.sigmoid(gate)
    activated = gate * logistic
    hidden[...] = (activated * up).astype(BF)
    act[...] = activated
    slope[...] = up * logistic * (1.0 + gate * (1.0 - logistic))


def forward(sc, rows, w_own, w_oth):
    tile = ROWS // 2
    line = lambda m, sc: (m, 0)
    return pl.pallas_call(
        forward_kernel,
        grid_spec=pltpu.PrefetchScalarGridSpec(
            num_scalar_prefetch=1,
            grid=(2,),
            in_specs=[
                pl.BlockSpec((tile, D), line),
                whole((1024, 2 * F)),
                whole((1024, 2 * F)),
            ],
            out_specs=[pl.BlockSpec((tile, F), line)] * 3,
        ),
        out_shape=[
            jax.ShapeDtypeStruct((ROWS, F), BF),
            jax.ShapeDtypeStruct((ROWS, F), F32),
            jax.ShapeDtypeStruct((ROWS, F), F32),
        ],
        compiler_params=params(),
        cost_estimate=cost(2 * ROWS * D * 2 * F, 16 * MIB),
    )(sc, rows, w_own, w_oth)


def backward_kernel(sc, *refs):
    arrived, (w_own, w_oth, hidden, act, slope, scaled, d_both, q_out) = refs[:8], refs[8:]
    y, z_lo, core, z_hi = sc[0], sc[1], sc[2], sc[3]
    row = lax.broadcasted_iota(jnp.int32, (4 * BLK, 4 * BLK), 0)
    col = lax.broadcasted_iota(jnp.int32, (4 * BLK, 4 * BLK), 1)

    def split(v, size):
        major = sum([(v >= size * n).astype(jnp.int32) for n in range(1, 4)])
        return major, v - size * major

    row_z, row_rest = split(row, BLK)
    row_y, row_s = split(row_rest, CAP)
    col_d, col_rest = split(col, BLK)
    col_z, col_s = split(col_rest, CAP)
    turn = (
        (row_z == col_z) & (row_s == col_s) & (row_y == ((y - col_d) & 3))
    ).astype(F32).astype(BF)
    for dc in range(2):
        from_core = core ^ dc
        for n in range(0, D, 512):
            table = jnp.concatenate(
                [arrived[4 * dc + k][:, n : n + 512] for k in range(4)], axis=0
            )
            moved = mm(turn, table).astype(BF)
            for z in range(4):
                place = (z % 2) * 4 + from_core * 2 + z // 2
                start = pl.multiple_of(place * BLK, 16)
                scaled[pl.ds(start, BLK), n : n + 512] = moved[z * BLK : (z + 1) * BLK, :]
    tile = ROWS // 2
    lane = lax.broadcasted_iota(jnp.int32, (tile, 128), 1)
    expert = ((y * 2 + z_lo) * 2 + core) * 2 + z_hi
    for m in range(2):
        part = slice(m * tile, (m + 1) * tile)
        total = jnp.zeros((tile, F), F32)
        for half, w in ((z_hi, w_own), (1 - z_hi, w_oth)):
            for i in range(4):
                start = pl.multiple_of(half * 1024 + i * 256, 256)
                total = total + mm(scaled[part, pl.ds(start, 256)], w[i], 1, 1)
        d_both[part, :] = jnp.concatenate(
            [(total * slope[part, :]).astype(BF), (total * act[part, :]).astype(BF)], axis=1
        )
        q = jnp.sum(total * hidden[part, :].astype(F32), axis=1, keepdims=True)
        q_out[part, :] = jnp.where(lane == expert, q, 0.0).astype(BF)


def backward(sc, arrived, w_own, w_oth, hidden, act, slope):
    vmem = pl.BlockSpec(memory_space=pltpu.VMEM)
    return pl.pallas_call(
        backward_kernel,
        in_specs=[pl.BlockSpec(memory_space=pltpu.SMEM)] + [vmem] * 13,
        out_specs=[vmem] * 3,
        out_shape=[
            jax.ShapeDtypeStruct((ROWS, D), BF),
            jax.ShapeDtypeStruct((ROWS, 2 * F), BF),
            jax.ShapeDtypeStruct((ROWS, 128), BF),
        ],
        compiler_params=params(),
        cost_estimate=cost(2 * ROWS * (D * F + 448 * D), 20 * MIB),
    )(sc, *arrived, w_own, w_oth, hidden, act, slope)


def grads_kernel(sc, rows, scaled, d_both, hidden, gate_up, down):
    gate_up[...] = mm(rows[...], d_both[...], 0, 0).astype(BF)
    down[...] = mm(hidden[...], scaled[...], 0, 0).astype(BF)


def grads(sc, rows, scaled, d_both, hidden, own):
    def column(i, sc):
        half = sc[3] if own else 1 - sc[3]
        return (0, half * 4 + i)

    line = lambda i, sc: (i, 0)
    return pl.pallas_call(
        grads_kernel,
        grid_spec=pltpu.PrefetchScalarGridSpec(
            num_scalar_prefetch=1,
            grid=(4,),
            in_specs=[
                pl.BlockSpec((ROWS, 256), column),
                pl.BlockSpec((ROWS, 256), column),
                whole((ROWS, 2 * F)),
                whole((ROWS, F)),
            ],
            out_specs=[pl.BlockSpec((256, 2 * F), line), pl.BlockSpec((F, 256), line)],
        ),
        out_shape=[
            jax.ShapeDtypeStruct((1024, 2 * F), BF),
            jax.ShapeDtypeStruct((4 * F, 256), BF),
        ],
        compiler_params=params(),
        cost_estimate=cost(2 * ROWS * 1024 * 3 * F, 12 * MIB),
    )(sc, rows, scaled, d_both, hidden)


def inputs_kernel(sc, d_both, q, w_own, w_oth, out):
    z_hi = sc[3]
    own = pl.multiple_of(z_hi * 1024, 1024)
    oth = pl.multiple_of((1 - z_hi) * 1024, 1024)
    out[:, pl.ds(own, 1024)] = mm(d_both[...], w_own[...], 1, 1).astype(BF)
    out[:, pl.ds(oth, 1024)] = mm(d_both[...], w_oth[...], 1, 1).astype(BF)
    out[:, D:] = q[...]


def input_grads(sc, d_both, q, w_own, w_oth):
    tile = ROWS // 2
    line = lambda m, sc: (m, 0)
    return pl.pallas_call(
        inputs_kernel,
        grid_spec=pltpu.PrefetchScalarGridSpec(
            num_scalar_prefetch=1,
            grid=(2,),
            in_specs=[
                pl.BlockSpec((tile, 2 * F), line),
                pl.BlockSpec((tile, 128), line),
                whole((1024, 2 * F)),
                whole((1024, 2 * F)),
            ],
            out_specs=pl.BlockSpec((tile, WIDE), line),
        ),
        out_shape=jax.ShapeDtypeStruct((ROWS, WIDE), BF),
        compiler_params=params(),
        cost_estimate=cost(2 * ROWS * D * 2 * F, 16 * MIB),
    )(sc, d_both, q, w_own, w_oth)


def combine_kernel(sel, rows, *outs):
    for start in range(0, WIDE, 512):
        end = min(start + 512, WIDE)
        part = mm(sel[...], rows[:, start:end], 0, 0).astype(BF)
        for d in range(4):
            outs[d][:, start:end] = part[d * TOK : (d + 1) * TOK, :]


def combine(sel, rows):
    return pl.pallas_call(
        combine_kernel,
        out_shape=[jax.ShapeDtypeStruct((TOK, WIDE), BF)] * 4,
        compiler_params=params(),
        cost_estimate=cost(2 * ROWS * 512 * WIDE, 8 * MIB),
    )(sel, rows)


def final_kernel(a, b, c, d, routes, probs, out, out_probs):
    total = (a[...].astype(F32) + b[...].astype(F32)) + (
        c[...].astype(F32) + d[...].astype(F32)
    )
    out[...] = total[:, :D].astype(BF)
    table = total[:, D:]
    lane = lax.broadcasted_iota(jnp.int32, (TOK, 128), 1)
    chosen = routes[...]
    weight = probs[...].astype(BF).astype(F32)
    for k in range(TOP):
        value = jnp.sum(
            jnp.where(lane == chosen[:, k : k + 1], table, 0.0), axis=1, keepdims=True
        )
        out_probs[:, k : k + 1] = value / weight[:, k : k + 1]


def final(parts, routes, probs):
    return pl.pallas_call(
        final_kernel,
        out_shape=[
            jax.ShapeDtypeStruct((TOK, D), BF),
            jax.ShapeDtypeStruct((TOK, TOP), F32),
        ],
        compiler_params=params(16),
        cost_estimate=cost(0, 3 * MIB),
    )(*parts, routes, probs)


def z_index(z):
    return (z % 2) * 2 + z // 2


def along_y(k):
    return [(y, (y + k) % 4) for y in range(4)]


def along_z(k):
    return [(z_index(z), z_index((z + k) % 4)) for z in range(4)]


def along_yc(k, dc):
    return [(y * 2 + c, ((y + k) % 4) * 2 + (c ^ dc)) for y in range(4) for c in range(2)]


def body(tokens, cotangent, routes, probs, w_gate_up, w_down):
    names = ("y", "zl", "c", "zh", "x")
    sc = jnp.stack([lax.axis_index(n) for n in names]).astype(jnp.int32)
    z_hi = sc[3]
    tok, cot = add_meta(tokens, cotangent, routes, probs)
    toks, cots = [tok], [cot]
    for k in (1, 2, 3):
        toks.append(lax.ppermute(tok, "y", along_y(k)))
        cots.append(lax.ppermute(cot, ("zl", "zh"), along_z(k)))

    pick_half = lambda w, i: lax.dynamic_index_in_dim(w, i, 0, keepdims=False)
    swap = [(0, 1), (1, 0)]
    own_gu, own_dn = pick_half(w_gate_up, z_hi), pick_half(w_down, z_hi)
    oth_gu = lax.ppermute(pick_half(w_gate_up, 1 - z_hi), "zh", swap)
    oth_dn = lax.ppermute(pick_half(w_down, 1 - z_hi), "zh", swap)
    gather = lambda w, t: lax.all_gather(w, "x", axis=0, tiled=t)
    gu_own, gu_oth = gather(own_gu, True), gather(oth_gu, True)
    dn_own, dn_oth = gather(own_dn, False), gather(oth_dn, False)

    x_send, sel = pick(pick_tokens_kernel, sc, toks, False)
    x_rows = lax.all_to_all(
        x_send.reshape(8, BLK, D), ("zl", "c", "zh"), split_axis=0, concat_axis=0, tiled=True
    ).reshape(ROWS, D)
    sent = pick(pick_cotan_kernel, sc, cots, True)
    arrived = [
        sent[j] if j == 0 else lax.ppermute(sent[j], ("y", "c"), along_yc(j % 4, j // 4))
        for j in range(8)
    ]
    hidden, act, slope = forward(sc, x_rows, gu_own, gu_oth)
    scaled, d_both, q = backward(sc, arrived, dn_own, dn_oth, hidden, act, slope)

    scatter = lambda g: lax.psum_scatter(g, "x", scatter_dimension=0, tiled=True)
    oth_part = grads(sc, x_rows, scaled, d_both, hidden, False)
    own_part = grads(sc, x_rows, scaled, d_both, hidden, True)
    oth_sum = [lax.ppermute(scatter(g), "zh", swap) for g in oth_part]
    own_sum = [scatter(g) for g in own_part]
    grad_gu, grad_dn = [
        jnp.where(z_hi == 0, jnp.stack([a, b]), jnp.stack([b, a]))
        for a, b in zip(own_sum, oth_sum)
    ]

    dx = input_grads(sc, d_both, q, gu_own, gu_oth)
    back = lax.all_to_all(
        dx.reshape(8, BLK, WIDE), ("zl", "c", "zh"), split_axis=0, concat_axis=0, tiled=True
    ).reshape(ROWS, WIDE)
    parts = combine(sel, back)
    parts = [parts[0]] + [lax.ppermute(parts[k], "y", along_y(-k)) for k in (1, 2, 3)]
    d_tokens, d_probs = final(parts, routes, probs)
    return d_tokens, d_probs, grad_gu, grad_dn


def solution(mesh):
    fine = Mesh(mesh.devices.reshape(4, 2, 2, 2, 4), ("y", "zl", "c", "zh", "x"))
    exp, fsdp = ("y", "zl", "c"), ("zh", "x")
    row = P(exp + fsdp, None)
    gate_up, down = P(exp, fsdp, None), P(exp, None, fsdp)
    return jax.shard_map(
        body,
        mesh=fine,
        in_specs=(row, row, row, row, gate_up, down),
        out_specs=(row, row, gate_up, down),
        check_vma=False,
    )
```

```python
import jax
import jax.numpy as jnp
from jax import lax
from jax.experimental import pallas as pl
from jax.experimental.pallas import tpu as pltpu
from jax.sharding import Mesh, PartitionSpec as P

TOP = 6
CAP = 28
SLOT = 32
EXPERTS = 32
D = 2048
F = 704
TOK = 128
WIDE = D + 128
PACK = 3 * F + 64
ROWS = 8 * 4 * CAP
BLK = 4 * CAP
BF = jnp.bfloat16
F32 = jnp.float32
MIB = 1 << 20
FINAL_FLOPS = 10**11


def params():
    return pltpu.CompilerParams(vmem_limit_bytes=60 * MIB)


def mm(a, b, ca=1, cb=0):
    return lax.dot_general(a, b, (((ca,), (cb,)), ((), ())), preferred_element_type=F32)


def whole(shape):
    return pl.BlockSpec(shape, lambda *_: (0,) * len(shape))


def cost(flops, moved):
    return pl.CostEstimate(flops=flops, bytes_accessed=moved, transcendentals=0)


def prepare_kernel(sc, tok, cot, routes, probs, gate_up, down, out_tok, out_cot, own, oth):
    z_hi = sc[3]
    line = lax.broadcasted_iota(jnp.int32, (128, TOK), 0)
    meta = jnp.zeros((128, TOK), F32)
    chosen = routes[...].astype(F32)
    weight = probs[...]
    for k in range(TOP):
        meta = jnp.where(line == k, chosen[k : k + 1, :], meta)
        meta = jnp.where(line == 8 + k, weight[k : k + 1, :], meta)
    meta = meta.T.astype(BF)
    for n in range(4):
        out_tok[n, :, :D] = tok[...]
        out_tok[n, :, D:] = meta
    out_cot[:, :D] = cot[...]
    out_cot[:, D:] = meta
    for out, which in ((own, z_hi), (oth, 1 - z_hi)):
        out[:, : 2 * F] = gate_up[which]
        out[:, 2 * F : 3 * F] = down[which].T
        out[:, 3 * F :] = jnp.zeros((256, PACK - 3 * F), BF)


def prepare(sc, tokens, cotangent, routes, probs, w_gate_up, w_down):
    vmem = pl.BlockSpec(memory_space=pltpu.VMEM)
    wide = jax.ShapeDtypeStruct((TOK, WIDE), BF)
    shard = jax.ShapeDtypeStruct((256, PACK), BF)
    return pl.pallas_call(
        prepare_kernel,
        in_specs=[pl.BlockSpec(memory_space=pltpu.SMEM)] + [vmem] * 6,
        out_specs=[vmem] * 4,
        out_shape=(jax.ShapeDtypeStruct((4, TOK, WIDE), BF), wide, shard, shard),
        compiler_params=params(),
        cost_estimate=cost(0, 8 * MIB),
    )(sc, tokens, cotangent, routes, probs, w_gate_up, w_down)


def pick_matrix(metas, experts, bases, weighted, sel):
    earlier = (
        lax.broadcasted_iota(jnp.int32, (TOK, TOK), 0)
        < lax.broadcasted_iota(jnp.int32, (TOK, TOK), 1)
    ).astype(BF)
    places, weights = [], []
    for d in range(4):
        turned = metas[d][...].astype(F32).T
        mask = jnp.zeros((8, TOK), F32)
        weight = jnp.zeros((8, TOK), F32)
        for k in range(TOP):
            hit = turned[k : k + 1, :] == experts
            mask = jnp.where(hit, 1.0, mask)
            weight = jnp.where(hit, turned[8 + k : 9 + k, :], weight)
        rank = mm(mask.astype(BF), earlier)
        places.append(jnp.where(mask > 0.5, rank + bases[d], -1.0))
        weights.append(weight if weighted else mask)
    place = jnp.concatenate(places, axis=1)
    weight = jnp.concatenate(weights, axis=1)
    row = lax.broadcasted_iota(jnp.int32, (BLK, 4 * TOK), 0).astype(F32)
    for j in range(8):
        sel[j * BLK : (j + 1) * BLK, :] = jnp.where(
            row == place[j : j + 1, :], weight[j : j + 1, :], 0.0
        ).astype(BF)


def pick_kernel(sc, *refs):
    x_tab, x_meta, c_tabs, c_metas = refs[0], refs[1], refs[2:6], refs[6:10]
    shard, x_out, shard_out = refs[10:13]
    c_outs, x_sel, c_sel = refs[13:21], refs[21], refs[22]
    y, z_lo, core, z_hi = sc[0], sc[1], sc[2], sc[3]
    z = z_hi * 2 + z_lo

    @pl.when(pl.program_id(0) == 0)
    def _():
        index = lax.broadcasted_iota(jnp.int32, (8, TOK), 0)
        bases = [float(n * CAP) for n in range(4)]
        x_metas = [x_meta.at[n] for n in range(4)]
        pick_matrix(x_metas, (y * 8 + index).astype(F32), bases, False, x_sel)
        experts = jnp.zeros((8, TOK), jnp.int32)
        for j in range(8):
            to_y, to_core = (y + j % 4) & 3, core ^ (j // 4)
            experts = jnp.where(
                index == j, ((to_y * 2 + z_lo) * 2 + to_core) * 2 + z_hi, experts
            )
        bases = [(((z - d) & 3) * CAP).astype(F32) for d in range(4)]
        pick_matrix(c_metas, experts.astype(F32), bases, True, c_sel)

    shard_out[...] = shard[...]
    x_out[...] = mm(x_sel[...], x_tab[...].reshape(4 * TOK, -1)).astype(BF)
    rows = mm(c_sel[...], jnp.concatenate([t[...] for t in c_tabs], axis=0)).astype(BF)
    for j in range(8):
        c_outs[j][...] = rows[j * BLK : (j + 1) * BLK, :]


def pick(sc, toks, cots, shard):
    step = 512
    column = lambda n, sc: (0, n)
    line = lambda n, sc: (n, 0)
    tables = [
        pl.BlockSpec((4, TOK, step), lambda n, sc: (0, 0, n)),
        pl.BlockSpec((4, TOK, 128), lambda n, sc: (0, 0, D // 128)),
    ]
    tables += [pl.BlockSpec((TOK, step), column)] * 4
    tables += [pl.BlockSpec((TOK, 128), lambda n, sc: (0, D // 128))] * 4
    outs = pl.pallas_call(
        pick_kernel,
        grid_spec=pltpu.PrefetchScalarGridSpec(
            num_scalar_prefetch=1,
            grid=(D // step,),
            in_specs=tables + [pl.BlockSpec((64, PACK), line)],
            out_specs=[
                pl.BlockSpec((ROWS, step), column),
                pl.BlockSpec((64, PACK), line),
            ]
            + [pl.BlockSpec((BLK, step), column)] * 8,
            scratch_shapes=[pltpu.VMEM((ROWS, 4 * TOK), BF)] * 2,
        ),
        out_shape=[
            jax.ShapeDtypeStruct((ROWS, D), BF),
            jax.ShapeDtypeStruct((256, PACK), BF),
        ]
        + [jax.ShapeDtypeStruct((BLK, D), BF)] * 8,
        compiler_params=params(),
        cost_estimate=cost(4 * ROWS * 512 * D, 16 * MIB),
    )(sc, toks, toks, *cots, *cots, shard)
    return outs[0], outs[1], outs[2:]


def expert_kernel(sc, *refs):
    arrived, (x_in, w_own, w_oth) = refs[:8], refs[8:11]
    scaled_out, d_both_out, hidden_out, q_out, grad_out = refs[11:16]
    x, table, w, scaled, d_both, hidden, act, slope, q_rows, grad = refs[16:26]
    sem_in, sem_out = refs[26:]
    y, z_lo, core, z_hi = sc[0], sc[1], sc[2], sc[3]
    tile = ROWS // 2
    loads, stores = [], []

    def fetch(src, dst):
        copy = pltpu.make_async_copy(src, dst, sem_in.at[len(loads)])
        copy.start()
        loads.append(copy)
        return copy

    def put(src, dst):
        copy = pltpu.make_async_copy(src, dst, sem_out.at[len(stores)])
        copy.start()
        stores.append(copy)

    own = pl.multiple_of(z_hi * 1024, 1024)
    oth = pl.multiple_of((1 - z_hi) * 1024, 1024)
    w_copies = [
        fetch(w_own, w.at[pl.ds(own, 1024)]),
        fetch(w_oth, w.at[pl.ds(oth, 1024)]),
    ]
    fetch_x = lambda m: fetch(
        x_in.at[pl.ds(m * tile, tile)], x.at[pl.ds(m * tile, tile)]
    )
    x_copies = [fetch_x(0)]
    lane = lax.broadcasted_iota(jnp.int32, (tile, 128), 1)
    expert = ((y * 2 + z_lo) * 2 + core) * 2 + z_hi

    for m in range(2):
        part = slice(m * tile, (m + 1) * tile)
        if m == 0:
            w_copies[0].wait()
            w_copies[1].wait()
            x_copies.append(fetch_x(1))
            c_copies = [
                fetch(arrived[j], table.at[pl.ds(j * BLK, BLK)]) for j in range(8)
            ]
        x_copies[m].wait()
        both = mm(x[part, :], w[:, : 2 * F])
        gate, up = both[:, :F], both[:, F:]
        logistic = jax.nn.sigmoid(gate)
        activated = gate * logistic
        hidden[part, :] = (activated * up).astype(BF)
        act[part, :] = activated
        slope[part, :] = up * logistic * (1.0 + gate * (1.0 - logistic))
    put(hidden, hidden_out)

    row = lax.broadcasted_iota(jnp.int32, (4 * BLK, 4 * BLK), 0)
    col = lax.broadcasted_iota(jnp.int32, (4 * BLK, 4 * BLK), 1)

    def split(v, size):
        major = sum([(v >= size * n).astype(jnp.int32) for n in range(1, 4)])
        return major, v - size * major

    row_z, row_rest = split(row, BLK)
    row_y, row_s = split(row_rest, CAP)
    col_d, col_rest = split(col, BLK)
    col_z, col_s = split(col_rest, CAP)
    turn = (
        (row_z == col_z) & (row_s == col_s) & (row_y == ((y - col_d) & 3))
    ).astype(F32).astype(BF)
    for copy in c_copies:
        copy.wait()
    for dc in range(2):
        from_core = core ^ dc
        for n in range(0, D, 512):
            moved = mm(turn, table[dc * 4 * BLK : (dc + 1) * 4 * BLK, n : n + 512]).astype(BF)
            for z in range(4):
                place = (z % 2) * 4 + from_core * 2 + z // 2
                start = pl.multiple_of(place * BLK, 16)
                scaled[pl.ds(start, BLK), n : n + 512] = moved[z * BLK : (z + 1) * BLK, :]
    put(scaled, scaled_out)

    for m in range(2):
        part = slice(m * tile, (m + 1) * tile)
        total = mm(scaled[part, :], w[:, 2 * F : 3 * F])
        d_both[part, :] = jnp.concatenate(
            [(total * slope[part, :]).astype(BF), (total * act[part, :]).astype(BF)], axis=1
        )
        q = jnp.sum(total * hidden[part, :].astype(F32), axis=1, keepdims=True)
        q_rows[part, :] = jnp.where(lane == expert, q, 0.0).astype(BF)
    put(d_both, d_both_out)
    put(q_rows, q_out)

    for i in range(4):
        start = pl.multiple_of(oth + i * 256, 256)
        line = slice(i * 256, (i + 1) * 256)
        grad[line, : 2 * F] = mm(x[:, pl.ds(start, 256)], d_both[...], 0, 0).astype(BF)
        grad[line, 2 * F : 3 * F] = mm(scaled[:, pl.ds(start, 256)], hidden[...], 0, 0).astype(BF)
        grad[line, 3 * F :] = jnp.zeros((256, PACK - 3 * F), BF)
        put(grad.at[pl.ds(i * 256, 256)], grad_out.at[pl.ds(i * 256, 256)])
    for copy in stores:
        copy.wait()


def expert_pass(sc, x_rows, arrived, w_own, w_oth):
    anywhere = pl.BlockSpec(memory_space=pl.ANY)
    shapes = [(ROWS, D), (ROWS, 2 * F), (ROWS, F), (ROWS, 128), (1024, PACK)]
    scratch = [
        ((ROWS, D), BF),
        ((ROWS, D), BF),
        ((D, PACK), BF),
        ((ROWS, D), BF),
        ((ROWS, 2 * F), BF),
        ((ROWS, F), BF),
        ((ROWS, F), F32),
        ((ROWS, F), F32),
        ((ROWS, 128), BF),
        ((1024, PACK), BF),
    ]
    return pl.pallas_call(
        expert_kernel,
        in_specs=[pl.BlockSpec(memory_space=pltpu.SMEM)] + [anywhere] * 11,
        out_specs=[anywhere] * 5,
        out_shape=[jax.ShapeDtypeStruct(shape, BF) for shape in shapes],
        scratch_shapes=[pltpu.VMEM(*item) for item in scratch]
        + [pltpu.SemaphoreType.DMA((12,)), pltpu.SemaphoreType.DMA((8,))],
        compiler_params=params(),
        cost_estimate=cost(2 * ROWS * D * 6 * F, 32 * MIB),
    )(sc, *arrived, x_rows, w_own, w_oth)


def inputs_kernel(sc, d_both_in, q, w_own, w_oth, dx_out, d_both, w, dx, sem_in, sem_out):
    z_hi = sc[3]
    tile = ROWS // 2
    own = pl.multiple_of(z_hi * 1024, 1024)
    oth = pl.multiple_of((1 - z_hi) * 1024, 1024)
    pairs = (
        (d_both_in, d_both),
        (w_own.at[:, pl.ds(0, 2 * F)], w.at[pl.ds(own, 1024)]),
        (w_oth.at[:, pl.ds(0, 2 * F)], w.at[pl.ds(oth, 1024)]),
    )
    loads = [pltpu.make_async_copy(*pair, sem_in.at[i]) for i, pair in enumerate(pairs)]
    stores = []
    for copy in loads:
        copy.start()
    extra = q[...].astype(F32)
    for copy in loads:
        copy.wait()
    for m in range(2):
        part = slice(m * tile, (m + 1) * tile)
        rows = mm(d_both[part, :], w[...], 1, 1)
        for to_y in range(4):
            for j in range(4):
                first, block = j * BLK + to_y * CAP, to_y * 8 + m * 4 + j
                dx[block, :, :D] = rows[first : first + CAP, :].astype(BF)
                first += m * tile
                dx[block, :, D:] = extra[first : first + CAP, :].astype(BF)
            span = pl.ds(to_y * 8 + m * 4, 4)
            copy = pltpu.make_async_copy(dx.at[span], dx_out.at[span], sem_out.at[len(stores)])
            copy.start()
            stores.append(copy)
    for copy in stores:
        copy.wait()


def input_grads(sc, d_both, q, w_own, w_oth):
    anywhere = pl.BlockSpec(memory_space=pl.ANY)
    scratch = [(ROWS, 2 * F), (D, 2 * F), (EXPERTS, CAP, WIDE)]
    return pl.pallas_call(
        inputs_kernel,
        in_specs=[
            pl.BlockSpec(memory_space=pltpu.SMEM),
            anywhere,
            pl.BlockSpec(memory_space=pltpu.VMEM),
            anywhere,
            anywhere,
        ],
        out_specs=anywhere,
        out_shape=jax.ShapeDtypeStruct((EXPERTS, CAP, WIDE), BF),
        scratch_shapes=[pltpu.VMEM(shape, BF) for shape in scratch]
        + [pltpu.SemaphoreType.DMA((3,)), pltpu.SemaphoreType.DMA((8,))],
        compiler_params=params(),
        cost_estimate=cost(2 * ROWS * D * 2 * F, 16 * MIB),
    )(sc, d_both, q, w_own, w_oth)


def grads_kernel(sc, x_in, scaled_in, d_both_in, hidden_in, grad_out, *refs):
    x, scaled, d_both, hidden, grad, sem_in, sem_out = refs
    own = pl.multiple_of(sc[3] * 1024, 1024)
    pairs = (
        (d_both_in, d_both),
        (x_in.at[:, pl.ds(own, 1024)], x),
        (hidden_in, hidden),
        (scaled_in.at[:, pl.ds(own, 1024)], scaled),
    )
    loads = [pltpu.make_async_copy(*pair, sem_in.at[i]) for i, pair in enumerate(pairs)]
    stores = []
    for copy in loads:
        copy.start()
    for copy in loads:
        copy.wait()
    for i in range(4):
        line = slice(i * 256, (i + 1) * 256)
        grad[line, : 2 * F] = mm(x[:, line], d_both[...], 0, 0).astype(BF)
        grad[line, 2 * F : 3 * F] = mm(scaled[:, line], hidden[...], 0, 0).astype(BF)
        grad[line, 3 * F :] = jnp.zeros((256, PACK - 3 * F), BF)
        span = pl.ds(i * 256, 256)
        copy = pltpu.make_async_copy(grad.at[span], grad_out.at[span], sem_out.at[i])
        copy.start()
        stores.append(copy)
    for copy in stores:
        copy.wait()


def own_grads(sc, x_rows, scaled, d_both, hidden):
    anywhere = pl.BlockSpec(memory_space=pl.ANY)
    scratch = [(ROWS, 1024), (ROWS, 1024), (ROWS, 2 * F), (ROWS, F), (1024, PACK)]
    return pl.pallas_call(
        grads_kernel,
        in_specs=[pl.BlockSpec(memory_space=pltpu.SMEM)] + [anywhere] * 4,
        out_specs=anywhere,
        out_shape=jax.ShapeDtypeStruct((1024, PACK), BF),
        scratch_shapes=[pltpu.VMEM(shape, BF) for shape in scratch]
        + [pltpu.SemaphoreType.DMA((4,)), pltpu.SemaphoreType.DMA((4,))],
        compiler_params=params(),
        cost_estimate=cost(2 * ROWS * 1024 * 3 * F, 12 * MIB),
    )(sc, x_rows, scaled, d_both, hidden)


def final_kernel(back, routes, probs, out, out_probs, sel, rows):
    experts = lax.broadcasted_iota(jnp.int32, (EXPERTS, TOK), 0)
    mask = jnp.zeros((EXPERTS, TOK), F32)
    for k in range(TOP):
        mask = jnp.where(routes[k : k + 1, :] == experts, 1.0, mask)
    earlier = (
        lax.broadcasted_iota(jnp.int32, (TOK, TOK), 0)
        < lax.broadcasted_iota(jnp.int32, (TOK, TOK), 1)
    ).astype(BF)
    place = jnp.where(mask > 0.5, mm(mask.astype(BF), earlier), -1.0)
    slot = lax.broadcasted_iota(jnp.int32, (SLOT, TOK), 0).astype(F32)
    for e in range(EXPERTS):
        line = slice(e * SLOT, (e + 1) * SLOT)
        sel[line, :] = (slot == place[e : e + 1, :]).astype(F32).astype(BF)
        rows[e, :CAP, :] = back[e]
        rows[e, CAP:, :] = jnp.zeros((SLOT - CAP, WIDE), BF)
    table = rows[...].reshape(EXPERTS * SLOT, WIDE)
    for n in range(0, D, 512):
        out[:, n : n + 512] = mm(sel[...], table[:, n : n + 512], 0, 0).astype(BF)
    values = mm(table[:, D:], sel[...], 0, 0)
    weight = probs[...].astype(BF).astype(F32)
    line = lax.broadcasted_iota(jnp.int32, (128, TOK), 0)
    for k in range(TOP):
        value = jnp.sum(
            jnp.where(line == routes[k : k + 1, :], values, 0.0), axis=0, keepdims=True
        )
        out_probs[k : k + 1, :] = value / weight[k : k + 1, :]


def final(back, routes, probs):
    return pl.pallas_call(
        final_kernel,
        out_shape=[
            jax.ShapeDtypeStruct((TOK, D), BF),
            jax.ShapeDtypeStruct((TOP, TOK), F32),
        ],
        scratch_shapes=[
            pltpu.VMEM((EXPERTS * SLOT, TOK), BF),
            pltpu.VMEM((EXPERTS, SLOT, WIDE), BF),
        ],
        compiler_params=params(),
        cost_estimate=cost(FINAL_FLOPS, 8 * MIB),
    )(back, routes, probs)


def place_kernel(sc, own, oth, gate_up, down, turned, sems):
    copies = []
    for i, (part, which) in enumerate(((oth, 1 - sc[3]), (own, sc[3]))):
        copy = pltpu.make_async_copy(
            part.at[:, pl.ds(0, 2 * F)], gate_up.at[which], sems.at[2 * i]
        )
        copy.start()
        turned[i] = part[:, 2 * F : 3 * F].T
        after = pltpu.make_async_copy(turned.at[i], down.at[which], sems.at[2 * i + 1])
        after.start()
        copies += [copy, after]
    for copy in copies:
        copy.wait()


def place(sc, own, oth):
    vmem = pl.BlockSpec(memory_space=pltpu.VMEM)
    return pl.pallas_call(
        place_kernel,
        in_specs=[pl.BlockSpec(memory_space=pltpu.SMEM), vmem, vmem],
        out_specs=[pl.BlockSpec(memory_space=pl.ANY)] * 2,
        out_shape=[
            jax.ShapeDtypeStruct((2, 256, 2 * F), BF),
            jax.ShapeDtypeStruct((2, F, 256), BF),
        ],
        scratch_shapes=[pltpu.VMEM((2, F, 256), BF), pltpu.SemaphoreType.DMA((4,))],
        compiler_params=params(),
        cost_estimate=cost(0, 5 * MIB),
    )(sc, own, oth)


def z_index(z):
    return (z % 2) * 2 + z // 2


def along_y(k):
    return [(y, (y + k) % 4) for y in range(4)]


def along_z(k):
    return [(z_index(z), z_index((z + k) % 4)) for z in range(4)]


def along_yc(k, dc):
    return [(y * 2 + c, ((y + k) % 4) * 2 + (c ^ dc)) for y in range(4) for c in range(2)]


def body(tokens, cotangent, routes, probs, w_gate_up, w_down):
    names = ("y", "zl", "c", "zh", "x")
    sc = jnp.stack([lax.axis_index(n) for n in names]).astype(jnp.int32)
    tok, cot, own, oth = prepare(
        sc, tokens, cotangent, routes.T, probs.T, w_gate_up, w_down
    )
    cots = [cot] + [lax.ppermute(cot, ("zl", "zh"), along_z(k)) for k in (1, 2, 3)]
    toks = lax.all_to_all(tok, "y", split_axis=0, concat_axis=0, tiled=True)
    swap = [(0, 1), (1, 0)]
    gather = lambda w: lax.all_gather(w, "x", axis=0, tiled=True)
    x_send, oth, sent = pick(sc, toks, cots, lax.ppermute(oth, "zh", swap))
    w_own, w_oth = gather(own), gather(oth)

    x_rows = lax.all_to_all(
        x_send.reshape(8, BLK, D), ("zl", "c", "zh"), split_axis=0, concat_axis=0, tiled=True
    ).reshape(ROWS, D)
    arrived = [
        sent[j] if j == 0 else lax.ppermute(sent[j], ("y", "c"), along_yc(j % 4, j // 4))
        for j in range(8)
    ]
    scaled, d_both, hidden, q, oth_part = expert_pass(sc, x_rows, arrived, w_own, w_oth)

    scatter = lambda g: lax.psum_scatter(g, "x", scatter_dimension=0, tiled=True)
    oth_sum = lax.ppermute(scatter(oth_part), "zh", swap)
    dx = input_grads(sc, d_both, q, w_own, w_oth)
    own_sum = scatter(own_grads(sc, x_rows, scaled, d_both, hidden))
    back = lax.all_to_all(
        dx, ("y", "zl", "c", "zh"), split_axis=0, concat_axis=0, tiled=True
    )
    d_tokens, d_probs = final(back, routes.T, probs.T)
    grad_gu, grad_dn = place(sc, own_sum, oth_sum)
    return d_tokens, d_probs.T, grad_gu, grad_dn


def solution(mesh):
    fine = Mesh(mesh.devices.reshape(4, 2, 2, 2, 4), ("y", "zl", "c", "zh", "x"))
    exp, fsdp = ("y", "zl", "c"), ("zh", "x")
    row = P(exp + fsdp, None)
    gate_up, down = P(exp, fsdp, None), P(exp, None, fsdp)
    return jax.shard_map(
        body,
        mesh=fine,
        in_specs=(row, row, row, row, gate_up, down),
        out_specs=(row, row, gate_up, down),
        check_vma=False,
    )
```

```python
import jax
import jax.numpy as jnp
from jax import lax
from jax.experimental import pallas as pl
from jax.experimental.pallas import tpu as pltpu
from jax.sharding import Mesh, PartitionSpec as P

TOP = 6
CAP = 28
SLOT = 32
EXPERTS = 32
D = 2048
F = 704
TOK = 128
WIDE = D + 128
PACK = 3 * F + 64
ROWS = 8 * 4 * CAP
BLK = 4 * CAP
BF = jnp.bfloat16
F32 = jnp.float32
MIB = 1 << 20
FINAL_FLOPS = 10**11


def params():
    return pltpu.CompilerParams(vmem_limit_bytes=63 * MIB)


def mm(a, b, ca=1, cb=0):
    return lax.dot_general(a, b, (((ca,), (cb,)), ((), ())), preferred_element_type=F32)


def whole(shape):
    return pl.BlockSpec(shape, lambda *_: (0,) * len(shape))


def cost(flops, moved):
    return pl.CostEstimate(flops=flops, bytes_accessed=moved, transcendentals=0)


def prepare_kernel(sc, tok, cot, routes, probs, gate_up, down, out_tok, out_cot, own, oth):
    z_hi = sc[3]
    line = lax.broadcasted_iota(jnp.int32, (128, TOK), 0)
    meta = jnp.zeros((128, TOK), F32)
    chosen = routes[...].astype(F32)
    weight = probs[...]
    for k in range(TOP):
        meta = jnp.where(line == k, chosen[k : k + 1, :], meta)
        meta = jnp.where(line == 8 + k, weight[k : k + 1, :], meta)
    meta = meta.T.astype(BF)
    for n in range(4):
        out_tok[n, :, :D] = tok[...]
        out_tok[n, :, D:] = meta
    out_cot[:, :D] = cot[...]
    out_cot[:, D:] = meta
    for out, which in ((own, z_hi), (oth, 1 - z_hi)):
        out[:, : 2 * F] = gate_up[which]
        out[:, 2 * F : 3 * F] = down[which].T
        out[:, 3 * F :] = jnp.zeros((256, PACK - 3 * F), BF)


def prepare(sc, tokens, cotangent, routes, probs, w_gate_up, w_down):
    vmem = pl.BlockSpec(memory_space=pltpu.VMEM)
    wide = jax.ShapeDtypeStruct((TOK, WIDE), BF)
    shard = jax.ShapeDtypeStruct((256, PACK), BF)
    return pl.pallas_call(
        prepare_kernel,
        in_specs=[pl.BlockSpec(memory_space=pltpu.SMEM)] + [vmem] * 6,
        out_specs=[vmem] * 4,
        out_shape=(jax.ShapeDtypeStruct((4, TOK, WIDE), BF), wide, shard, shard),
        compiler_params=params(),
        cost_estimate=cost(0, 8 * MIB),
    )(sc, tokens, cotangent, routes, probs, w_gate_up, w_down)


def pick_matrix(metas, experts, bases, weighted, sel):
    earlier = (
        lax.broadcasted_iota(jnp.int32, (TOK, TOK), 0)
        < lax.broadcasted_iota(jnp.int32, (TOK, TOK), 1)
    ).astype(BF)
    places, weights = [], []
    for d in range(4):
        turned = metas[d][...].astype(F32).T
        mask = jnp.zeros((8, TOK), F32)
        weight = jnp.zeros((8, TOK), F32)
        for k in range(TOP):
            hit = turned[k : k + 1, :] == experts
            mask = jnp.where(hit, 1.0, mask)
            weight = jnp.where(hit, turned[8 + k : 9 + k, :], weight)
        rank = mm(mask.astype(BF), earlier)
        places.append(jnp.where(mask > 0.5, rank + bases[d], -1.0))
        weights.append(weight if weighted else mask)
    place = jnp.concatenate(places, axis=1)
    weight = jnp.concatenate(weights, axis=1)
    row = lax.broadcasted_iota(jnp.int32, (BLK, 4 * TOK), 0).astype(F32)
    for j in range(8):
        sel[j * BLK : (j + 1) * BLK, :] = jnp.where(
            row == place[j : j + 1, :], weight[j : j + 1, :], 0.0
        ).astype(BF)


def pick_kernel(sc, *refs):
    x_tab, x_meta, c_tabs, c_metas = refs[0], refs[1], refs[2:6], refs[6:10]
    x_out, c_outs, x_sel, c_sel = refs[10], refs[11:19], refs[19], refs[20]
    y, z_lo, core, z_hi = sc[0], sc[1], sc[2], sc[3]
    z = z_hi * 2 + z_lo

    @pl.when(pl.program_id(0) == 0)
    def _():
        index = lax.broadcasted_iota(jnp.int32, (8, TOK), 0)
        bases = [float(n * CAP) for n in range(4)]
        x_metas = [x_meta.at[n] for n in range(4)]
        pick_matrix(x_metas, (y * 8 + index).astype(F32), bases, False, x_sel)
        experts = jnp.zeros((8, TOK), jnp.int32)
        for j in range(8):
            to_y, to_core = (y + j % 4) & 3, core ^ (j // 4)
            experts = jnp.where(
                index == j, ((to_y * 2 + z_lo) * 2 + to_core) * 2 + z_hi, experts
            )
        bases = [(((z - d) & 3) * CAP).astype(F32) for d in range(4)]
        pick_matrix(c_metas, experts.astype(F32), bases, True, c_sel)

    x_out[...] = mm(x_sel[...], x_tab[...].reshape(4 * TOK, -1)).astype(BF)
    rows = mm(c_sel[...], jnp.concatenate([t[...] for t in c_tabs], axis=0)).astype(BF)
    for j in range(8):
        c_outs[j][...] = rows[j * BLK : (j + 1) * BLK, :]


def pick(sc, toks, cots):
    step = 512
    column = lambda n, sc: (0, n)
    tables = [
        pl.BlockSpec((4, TOK, step), lambda n, sc: (0, 0, n)),
        pl.BlockSpec((4, TOK, 128), lambda n, sc: (0, 0, D // 128)),
    ]
    tables += [pl.BlockSpec((TOK, step), column)] * 4
    tables += [pl.BlockSpec((TOK, 128), lambda n, sc: (0, D // 128))] * 4
    outs = pl.pallas_call(
        pick_kernel,
        grid_spec=pltpu.PrefetchScalarGridSpec(
            num_scalar_prefetch=1,
            grid=(D // step,),
            in_specs=tables,
            out_specs=[
                pl.BlockSpec((ROWS, step), column),
            ]
            + [pl.BlockSpec((BLK, step), column)] * 8,
            scratch_shapes=[pltpu.VMEM((ROWS, 4 * TOK), BF)] * 2,
        ),
        out_shape=[
            jax.ShapeDtypeStruct((ROWS, D), BF),
        ]
        + [jax.ShapeDtypeStruct((BLK, D), BF)] * 8,
        compiler_params=params(),
        cost_estimate=cost(4 * ROWS * 512 * D, 16 * MIB),
    )(sc, toks, toks, *cots, *cots)
    return outs[0], outs[1:]


def expert_kernel(sc, *refs):
    arrived, (x_in, w_own, w_oth) = refs[:8], refs[8:11]
    scaled_out, d_both_out, hidden_out, q_out, grad_out = refs[11:16]
    x, table, w, scaled, d_both, hidden, act, slope, q_rows, grad = refs[16:26]
    sem_in, sem_out = refs[26:]
    y, z_lo, core, z_hi = sc[0], sc[1], sc[2], sc[3]
    tile = ROWS // 2
    loads, stores = [], []

    def fetch(src, dst):
        copy = pltpu.make_async_copy(src, dst, sem_in.at[len(loads)])
        copy.start()
        loads.append(copy)
        return copy

    def put(src, dst):
        copy = pltpu.make_async_copy(src, dst, sem_out.at[len(stores)])
        copy.start()
        stores.append(copy)

    own = pl.multiple_of(z_hi * 1024, 1024)
    oth = pl.multiple_of((1 - z_hi) * 1024, 1024)
    w_copies = [
        fetch(w_own, w.at[pl.ds(own, 1024)]),
        fetch(w_oth, w.at[pl.ds(oth, 1024)]),
    ]
    fetch_x = lambda m: fetch(
        x_in.at[pl.ds(m * tile, tile)], x.at[pl.ds(m * tile, tile)]
    )
    x_copies = [fetch_x(0)]
    lane = lax.broadcasted_iota(jnp.int32, (tile, 128), 1)
    expert = ((y * 2 + z_lo) * 2 + core) * 2 + z_hi

    for m in range(2):
        part = slice(m * tile, (m + 1) * tile)
        if m == 0:
            w_copies[0].wait()
            w_copies[1].wait()
            x_copies.append(fetch_x(1))
            c_copies = [
                fetch(arrived[j], table.at[pl.ds(j * BLK, BLK)]) for j in range(8)
            ]
        x_copies[m].wait()
        both = mm(x[part, :], w[:, : 2 * F])
        gate, up = both[:, :F], both[:, F:]
        logistic = jax.nn.sigmoid(gate)
        activated = gate * logistic
        hidden[part, :] = (activated * up).astype(BF)
        act[part, :] = activated
        slope[part, :] = up * logistic * (1.0 + gate * (1.0 - logistic))
    put(hidden, hidden_out)

    row = lax.broadcasted_iota(jnp.int32, (4 * BLK, 4 * BLK), 0)
    col = lax.broadcasted_iota(jnp.int32, (4 * BLK, 4 * BLK), 1)

    def split(v, size):
        major = sum([(v >= size * n).astype(jnp.int32) for n in range(1, 4)])
        return major, v - size * major

    row_z, row_rest = split(row, BLK)
    row_y, row_s = split(row_rest, CAP)
    col_d, col_rest = split(col, BLK)
    col_z, col_s = split(col_rest, CAP)
    turn = (
        (row_z == col_z) & (row_s == col_s) & (row_y == ((y - col_d) & 3))
    ).astype(F32).astype(BF)
    for copy in c_copies:
        copy.wait()
    for dc in range(2):
        from_core = core ^ dc
        for n in range(0, D, 512):
            moved = mm(turn, table[dc * 4 * BLK : (dc + 1) * 4 * BLK, n : n + 512]).astype(BF)
            for z in range(4):
                place = (z % 2) * 4 + from_core * 2 + z // 2
                start = pl.multiple_of(place * BLK, 16)
                scaled[pl.ds(start, BLK), n : n + 512] = moved[z * BLK : (z + 1) * BLK, :]
    put(scaled, scaled_out)

    for m in range(2):
        part = slice(m * tile, (m + 1) * tile)
        total = mm(scaled[part, :], w[:, 2 * F : 3 * F])
        d_both[part, :] = jnp.concatenate(
            [(total * slope[part, :]).astype(BF), (total * act[part, :]).astype(BF)], axis=1
        )
        q = jnp.sum(total * hidden[part, :].astype(F32), axis=1, keepdims=True)
        q_rows[part, :] = jnp.where(lane == expert, q, 0.0).astype(BF)
    put(d_both, d_both_out)
    put(q_rows, q_out)

    for i in range(4):
        start = pl.multiple_of(oth + i * 256, 256)
        line = slice(i * 256, (i + 1) * 256)
        grad[line, : 2 * F] = mm(x[:, pl.ds(start, 256)], d_both[...], 0, 0).astype(BF)
        grad[line, 2 * F : 3 * F] = mm(scaled[:, pl.ds(start, 256)], hidden[...], 0, 0).astype(BF)
        grad[line, 3 * F :] = jnp.zeros((256, PACK - 3 * F), BF)
        put(grad.at[pl.ds(i * 256, 256)], grad_out.at[pl.ds(i * 256, 256)])
    for copy in stores:
        copy.wait()


def expert_pass(sc, x_rows, arrived, w_own, w_oth):
    anywhere = pl.BlockSpec(memory_space=pl.ANY)
    shapes = [(ROWS, D), (ROWS, 2 * F), (ROWS, F), (ROWS, 128), (1024, PACK)]
    scratch = [
        ((ROWS, D), BF),
        ((ROWS, D), BF),
        ((D, PACK), BF),
        ((ROWS, D), BF),
        ((ROWS, 2 * F), BF),
        ((ROWS, F), BF),
        ((ROWS, F), F32),
        ((ROWS, F), F32),
        ((ROWS, 128), BF),
        ((1024, PACK), BF),
    ]
    return pl.pallas_call(
        expert_kernel,
        in_specs=[pl.BlockSpec(memory_space=pltpu.SMEM)] + [anywhere] * 11,
        out_specs=[anywhere] * 5,
        out_shape=[jax.ShapeDtypeStruct(shape, BF) for shape in shapes],
        scratch_shapes=[pltpu.VMEM(*item) for item in scratch]
        + [pltpu.SemaphoreType.DMA((12,)), pltpu.SemaphoreType.DMA((8,))],
        compiler_params=params(),
        cost_estimate=cost(2 * ROWS * D * 6 * F, 32 * MIB),
    )(sc, *arrived, x_rows, w_own, w_oth)


def inputs_kernel(sc, d_both_in, q, w_own, w_oth, dx_out, d_both, w, dx, sem_in, sem_out):
    z_hi = sc[3]
    tile = ROWS // 2
    own = pl.multiple_of(z_hi * 1024, 1024)
    oth = pl.multiple_of((1 - z_hi) * 1024, 1024)
    pairs = (
        (d_both_in, d_both),
        (w_own.at[:, pl.ds(0, 2 * F)], w.at[pl.ds(own, 1024)]),
        (w_oth.at[:, pl.ds(0, 2 * F)], w.at[pl.ds(oth, 1024)]),
    )
    loads = [pltpu.make_async_copy(*pair, sem_in.at[i]) for i, pair in enumerate(pairs)]
    stores = []
    for copy in loads:
        copy.start()
    extra = q[...].astype(F32)
    for copy in loads:
        copy.wait()
    for m in range(2):
        part = slice(m * tile, (m + 1) * tile)
        rows = mm(d_both[part, :], w[...], 1, 1)
        for to_y in range(4):
            for j in range(4):
                first, block = j * BLK + to_y * CAP, to_y * 8 + m * 4 + j
                dx[block, :, :D] = rows[first : first + CAP, :].astype(BF)
                first += m * tile
                dx[block, :, D:] = extra[first : first + CAP, :].astype(BF)
            span = pl.ds(to_y * 8 + m * 4, 4)
            copy = pltpu.make_async_copy(dx.at[span], dx_out.at[span], sem_out.at[len(stores)])
            copy.start()
            stores.append(copy)
    for copy in stores:
        copy.wait()


def input_grads(sc, d_both, q, w_own, w_oth):
    anywhere = pl.BlockSpec(memory_space=pl.ANY)
    scratch = [(ROWS, 2 * F), (D, 2 * F), (EXPERTS, CAP, WIDE)]
    return pl.pallas_call(
        inputs_kernel,
        in_specs=[
            pl.BlockSpec(memory_space=pltpu.SMEM),
            anywhere,
            pl.BlockSpec(memory_space=pltpu.VMEM),
            anywhere,
            anywhere,
        ],
        out_specs=anywhere,
        out_shape=jax.ShapeDtypeStruct((EXPERTS, CAP, WIDE), BF),
        scratch_shapes=[pltpu.VMEM(shape, BF) for shape in scratch]
        + [pltpu.SemaphoreType.DMA((3,)), pltpu.SemaphoreType.DMA((8,))],
        compiler_params=params(),
        cost_estimate=cost(2 * ROWS * D * 2 * F, 16 * MIB),
    )(sc, d_both, q, w_own, w_oth)


def grads_kernel(sc, x_in, scaled_in, d_both_in, hidden_in, grad_out, *refs):
    x, scaled, d_both, hidden, grad, sem_in, sem_out = refs
    own = pl.multiple_of(sc[3] * 1024, 1024)
    pairs = (
        (d_both_in, d_both),
        (x_in.at[:, pl.ds(own, 1024)], x),
        (hidden_in, hidden),
        (scaled_in.at[:, pl.ds(own, 1024)], scaled),
    )
    loads = [pltpu.make_async_copy(*pair, sem_in.at[i]) for i, pair in enumerate(pairs)]
    stores = []
    for copy in loads:
        copy.start()
    for copy in loads:
        copy.wait()
    for i in range(4):
        line = slice(i * 256, (i + 1) * 256)
        grad[line, : 2 * F] = mm(x[:, line], d_both[...], 0, 0).astype(BF)
        grad[line, 2 * F : 3 * F] = mm(scaled[:, line], hidden[...], 0, 0).astype(BF)
        grad[line, 3 * F :] = jnp.zeros((256, PACK - 3 * F), BF)
        span = pl.ds(i * 256, 256)
        copy = pltpu.make_async_copy(grad.at[span], grad_out.at[span], sem_out.at[i])
        copy.start()
        stores.append(copy)
    for copy in stores:
        copy.wait()


def own_grads(sc, x_rows, scaled, d_both, hidden):
    anywhere = pl.BlockSpec(memory_space=pl.ANY)
    scratch = [(ROWS, 1024), (ROWS, 1024), (ROWS, 2 * F), (ROWS, F), (1024, PACK)]
    return pl.pallas_call(
        grads_kernel,
        in_specs=[pl.BlockSpec(memory_space=pltpu.SMEM)] + [anywhere] * 4,
        out_specs=anywhere,
        out_shape=jax.ShapeDtypeStruct((1024, PACK), BF),
        scratch_shapes=[pltpu.VMEM(shape, BF) for shape in scratch]
        + [pltpu.SemaphoreType.DMA((4,)), pltpu.SemaphoreType.DMA((4,))],
        compiler_params=params(),
        cost_estimate=cost(2 * ROWS * 1024 * 3 * F, 12 * MIB),
    )(sc, x_rows, scaled, d_both, hidden)


def hold_kernel(value, *rest):
    pass


def hold(value, *after):
    anywhere = pl.BlockSpec(memory_space=pl.ANY)
    return pl.pallas_call(
        hold_kernel,
        in_specs=[anywhere] * (1 + len(after)),
        out_specs=anywhere,
        out_shape=jax.ShapeDtypeStruct(value.shape, value.dtype),
        input_output_aliases={0: 0},
        compiler_params=params(),
    )(value, *after)


def final_kernel(back, routes, probs, out, out_probs, sel, rows):
    experts = lax.broadcasted_iota(jnp.int32, (EXPERTS, TOK), 0)
    mask = jnp.zeros((EXPERTS, TOK), F32)
    for k in range(TOP):
        mask = jnp.where(routes[k : k + 1, :] == experts, 1.0, mask)
    earlier = (
        lax.broadcasted_iota(jnp.int32, (TOK, TOK), 0)
        < lax.broadcasted_iota(jnp.int32, (TOK, TOK), 1)
    ).astype(BF)
    place = jnp.where(mask > 0.5, mm(mask.astype(BF), earlier), -1.0)
    slot = lax.broadcasted_iota(jnp.int32, (SLOT, TOK), 0).astype(F32)
    for e in range(EXPERTS):
        line = slice(e * SLOT, (e + 1) * SLOT)
        sel[line, :] = (slot == place[e : e + 1, :]).astype(F32).astype(BF)
        rows[e, :CAP, :] = back[e]
        rows[e, CAP:, :] = jnp.zeros((SLOT - CAP, WIDE), BF)
    table = rows[...].reshape(EXPERTS * SLOT, WIDE)
    for n in range(0, D, 512):
        out[:, n : n + 512] = mm(sel[...], table[:, n : n + 512], 0, 0).astype(BF)
    values = mm(table[:, D:], sel[...], 0, 0)
    weight = probs[...].astype(BF).astype(F32)
    line = lax.broadcasted_iota(jnp.int32, (128, TOK), 0)
    for k in range(TOP):
        value = jnp.sum(
            jnp.where(line == routes[k : k + 1, :], values, 0.0), axis=0, keepdims=True
        )
        out_probs[k : k + 1, :] = value / weight[k : k + 1, :]


def final(back, routes, probs):
    return pl.pallas_call(
        final_kernel,
        out_shape=[
            jax.ShapeDtypeStruct((TOK, D), BF),
            jax.ShapeDtypeStruct((TOP, TOK), F32),
        ],
        scratch_shapes=[
            pltpu.VMEM((EXPERTS * SLOT, TOK), BF),
            pltpu.VMEM((EXPERTS, SLOT, WIDE), BF),
        ],
        compiler_params=params(),
        cost_estimate=cost(FINAL_FLOPS, 8 * MIB),
    )(back, routes, probs)


def place_kernel(sc, own, oth, gate_up, down, turned, sems):
    copies = []
    for i, (part, which) in enumerate(((oth, 1 - sc[3]), (own, sc[3]))):
        copy = pltpu.make_async_copy(
            part.at[:, pl.ds(0, 2 * F)], gate_up.at[which], sems.at[2 * i]
        )
        copy.start()
        turned[i] = part[:, 2 * F : 3 * F].T
        after = pltpu.make_async_copy(turned.at[i], down.at[which], sems.at[2 * i + 1])
        after.start()
        copies += [copy, after]
    for copy in copies:
        copy.wait()


def place(sc, own, oth):
    vmem = pl.BlockSpec(memory_space=pltpu.VMEM)
    return pl.pallas_call(
        place_kernel,
        in_specs=[pl.BlockSpec(memory_space=pltpu.SMEM), vmem, vmem],
        out_specs=[pl.BlockSpec(memory_space=pl.ANY)] * 2,
        out_shape=[
            jax.ShapeDtypeStruct((2, 256, 2 * F), BF),
            jax.ShapeDtypeStruct((2, F, 256), BF),
        ],
        scratch_shapes=[pltpu.VMEM((2, F, 256), BF), pltpu.SemaphoreType.DMA((4,))],
        compiler_params=params(),
        cost_estimate=cost(0, 5 * MIB),
    )(sc, own, oth)


def z_index(z):
    return (z % 2) * 2 + z // 2


def along_y(k):
    return [(y, (y + k) % 4) for y in range(4)]


def along_z(k):
    return [(z_index(z), z_index((z + k) % 4)) for z in range(4)]


def along_yc(k, dc):
    return [(y * 2 + c, ((y + k) % 4) * 2 + (c ^ dc)) for y in range(4) for c in range(2)]


def body(tokens, cotangent, routes, probs, w_gate_up, w_down):
    names = ("y", "zl", "c", "zh", "x")
    sc = jnp.stack([lax.axis_index(n) for n in names]).astype(jnp.int32)
    tok, cot, own, oth = prepare(
        sc, tokens, cotangent, routes.T, probs.T, w_gate_up, w_down
    )
    cots = [cot] + [lax.ppermute(cot, ("zl", "zh"), along_z(k)) for k in (1, 2, 3)]
    toks = lax.all_to_all(tok, "y", split_axis=0, concat_axis=0, tiled=True)
    swap = [(0, 1), (1, 0)]
    gather = lambda w: lax.all_gather(w, "x", axis=0, tiled=True)
    oth = hold(lax.ppermute(oth, "zh", swap), toks, *cots[1:])
    x_send, sent = pick(sc, toks, cots)
    w_own, w_oth = gather(own), gather(oth)

    x_rows = lax.all_to_all(
        x_send.reshape(8, BLK, D), ("zl", "c", "zh"), split_axis=0, concat_axis=0, tiled=True
    ).reshape(ROWS, D)
    arrived = [
        sent[j] if j == 0 else lax.ppermute(sent[j], ("y", "c"), along_yc(j % 4, j // 4))
        for j in range(8)
    ]
    scaled, d_both, hidden, q, oth_part = expert_pass(sc, x_rows, arrived, w_own, w_oth)

    scatter = lambda g: lax.psum_scatter(g, "x", scatter_dimension=0, tiled=True)
    oth_sum = lax.ppermute(scatter(oth_part), "zh", swap)
    dx = input_grads(sc, d_both, q, w_own, w_oth)
    own_sum = scatter(own_grads(sc, x_rows, scaled, d_both, hidden))
    back = lax.all_to_all(
        dx, ("y", "zl", "c", "zh"), split_axis=0, concat_axis=0, tiled=True
    )
    d_tokens, d_probs = final(back, routes.T, probs.T)
    grad_gu, grad_dn = place(sc, own_sum, oth_sum)
    return d_tokens, d_probs.T, grad_gu, grad_dn


def solution(mesh):
    fine = Mesh(mesh.devices.reshape(4, 2, 2, 2, 4), ("y", "zl", "c", "zh", "x"))
    exp, fsdp = ("y", "zl", "c"), ("zh", "x")
    row = P(exp + fsdp, None)
    gate_up, down = P(exp, fsdp, None), P(exp, None, fsdp)
    return jax.shard_map(
        body,
        mesh=fine,
        in_specs=(row, row, row, row, gate_up, down),
        out_specs=(row, row, gate_up, down),
        check_vma=False,
    )
```

```python
import jax
import jax.numpy as jnp
from jax import lax
from jax.experimental import pallas as pl
from jax.experimental.pallas import tpu as pltpu
from jax.sharding import Mesh, PartitionSpec as P

TOP = 6
CAP = 28
SLOT = 32
EXPERTS = 32
D = 2048
F = 704
TOK = 128
WIDE = D + 128
PACK = 3 * F + 64
ROWS = 8 * 4 * CAP
BLK = 4 * CAP
BF = jnp.bfloat16
F32 = jnp.float32
MIB = 1 << 20
FINAL_FLOPS = 10**11


def params():
    return pltpu.CompilerParams(vmem_limit_bytes=63 * MIB)


def mm(a, b, ca=1, cb=0):
    return lax.dot_general(a, b, (((ca,), (cb,)), ((), ())), preferred_element_type=F32)


def whole(shape):
    return pl.BlockSpec(shape, lambda *_: (0,) * len(shape))


def cost(flops, moved):
    return pl.CostEstimate(flops=flops, bytes_accessed=moved, transcendentals=0)


def prepare_kernel(sc, tok, cot, routes, probs, gate_up, down, *refs):
    out_tok, out_cot, own, oth, tok_row, cot_row, packed, sems = refs
    copies = []

    def put(src, dst):
        copy = pltpu.make_async_copy(src, dst, sems.at[len(copies)])
        copy.start()
        copies.append(copy)

    z_hi = sc[3]
    line = lax.broadcasted_iota(jnp.int32, (128, TOK), 0)
    meta = jnp.zeros((128, TOK), F32)
    chosen = routes[...].astype(F32)
    weight = probs[...]
    for k in range(TOP):
        meta = jnp.where(line == k, chosen[k : k + 1, :], meta)
        meta = jnp.where(line == 8 + k, weight[k : k + 1, :], meta)
    meta = meta.T.astype(BF)
    tok_row[:, :D] = tok[...]
    tok_row[:, D:] = meta
    for n in range(4):
        put(tok_row, out_tok.at[n])
    cot_row[:, :D] = cot[...]
    cot_row[:, D:] = meta
    put(cot_row, out_cot)
    for i, (out, which) in enumerate(((own, z_hi), (oth, 1 - z_hi))):
        packed[i, :, : 2 * F] = gate_up[which]
        packed[i, :, 2 * F : 3 * F] = down[which].T
        packed[i, :, 3 * F :] = jnp.zeros((256, PACK - 3 * F), BF)
        put(packed.at[i], out)
    for copy in copies:
        copy.wait()


def prepare(sc, tokens, cotangent, routes, probs, w_gate_up, w_down):
    vmem = pl.BlockSpec(memory_space=pltpu.VMEM)
    wide = jax.ShapeDtypeStruct((TOK, WIDE), BF)
    shard = jax.ShapeDtypeStruct((256, PACK), BF)
    return pl.pallas_call(
        prepare_kernel,
        in_specs=[pl.BlockSpec(memory_space=pltpu.SMEM)] + [vmem] * 6,
        out_specs=[pl.BlockSpec(memory_space=pl.ANY)] * 4,
        out_shape=(jax.ShapeDtypeStruct((4, TOK, WIDE), BF), wide, shard, shard),
        scratch_shapes=[
            pltpu.VMEM((TOK, WIDE), BF),
            pltpu.VMEM((TOK, WIDE), BF),
            pltpu.VMEM((2, 256, PACK), BF),
            pltpu.SemaphoreType.DMA((7,)),
        ],
        compiler_params=params(),
        cost_estimate=cost(0, 8 * MIB),
    )(sc, tokens, cotangent, routes, probs, w_gate_up, w_down)


def pick_matrix(metas, experts, bases, weighted, sel):
    earlier = (
        lax.broadcasted_iota(jnp.int32, (TOK, TOK), 0)
        < lax.broadcasted_iota(jnp.int32, (TOK, TOK), 1)
    ).astype(BF)
    places, weights = [], []
    for d in range(4):
        turned = metas[d][...].astype(F32).T
        mask = jnp.zeros((8, TOK), F32)
        weight = jnp.zeros((8, TOK), F32)
        for k in range(TOP):
            hit = turned[k : k + 1, :] == experts
            mask = jnp.where(hit, 1.0, mask)
            weight = jnp.where(hit, turned[8 + k : 9 + k, :], weight)
        rank = mm(mask.astype(BF), earlier)
        places.append(jnp.where(mask > 0.5, rank + bases[d], -1.0))
        weights.append(weight if weighted else mask)
    place = jnp.concatenate(places, axis=1)
    weight = jnp.concatenate(weights, axis=1)
    row = lax.broadcasted_iota(jnp.int32, (BLK, 4 * TOK), 0).astype(F32)
    for j in range(8):
        sel[j * BLK : (j + 1) * BLK, :] = jnp.where(
            row == place[j : j + 1, :], weight[j : j + 1, :], 0.0
        ).astype(BF)


def pick_kernel(sc, *refs):
    x_tab, x_meta, c_tabs, c_metas = refs[0], refs[1], refs[2:6], refs[6:10]
    x_out, c_outs, x_sel, c_sel = refs[10], refs[11:19], refs[19], refs[20]
    y, z_lo, core, z_hi = sc[0], sc[1], sc[2], sc[3]
    z = z_hi * 2 + z_lo

    @pl.when(pl.program_id(0) == 0)
    def _():
        index = lax.broadcasted_iota(jnp.int32, (8, TOK), 0)
        bases = [float(n * CAP) for n in range(4)]
        x_metas = [x_meta.at[n] for n in range(4)]
        pick_matrix(x_metas, (y * 8 + index).astype(F32), bases, False, x_sel)
        experts = jnp.zeros((8, TOK), jnp.int32)
        for j in range(8):
            to_y, to_core = (y + j % 4) & 3, core ^ (j // 4)
            experts = jnp.where(
                index == j, ((to_y * 2 + z_lo) * 2 + to_core) * 2 + z_hi, experts
            )
        bases = [(((z - d) & 3) * CAP).astype(F32) for d in range(4)]
        pick_matrix(c_metas, experts.astype(F32), bases, True, c_sel)

    x_out[...] = mm(x_sel[...], x_tab[...].reshape(4 * TOK, -1)).astype(BF)
    rows = mm(c_sel[...], jnp.concatenate([t[...] for t in c_tabs], axis=0)).astype(BF)
    for j in range(8):
        c_outs[j][...] = rows[j * BLK : (j + 1) * BLK, :]


def pick(sc, toks, cots):
    step = 1024
    column = lambda n, sc: (0, n)
    tables = [
        pl.BlockSpec((4, TOK, step), lambda n, sc: (0, 0, n)),
        pl.BlockSpec((4, TOK, 128), lambda n, sc: (0, 0, D // 128)),
    ]
    tables += [pl.BlockSpec((TOK, step), column)] * 4
    tables += [pl.BlockSpec((TOK, 128), lambda n, sc: (0, D // 128))] * 4
    outs = pl.pallas_call(
        pick_kernel,
        grid_spec=pltpu.PrefetchScalarGridSpec(
            num_scalar_prefetch=1,
            grid=(D // step,),
            in_specs=tables,
            out_specs=[
                pl.BlockSpec((ROWS, step), column),
            ]
            + [pl.BlockSpec((BLK, step), column)] * 8,
            scratch_shapes=[pltpu.VMEM((ROWS, 4 * TOK), BF)] * 2,
        ),
        out_shape=[
            jax.ShapeDtypeStruct((ROWS, D), BF),
        ]
        + [jax.ShapeDtypeStruct((BLK, D), BF)] * 8,
        compiler_params=params(),
        cost_estimate=cost(4 * ROWS * 512 * D, 16 * MIB),
    )(sc, toks, toks, *cots, *cots)
    return outs[0], outs[1:]


def expert_kernel(sc, *refs):
    arrived, (x_in, w_own, w_oth) = refs[:8], refs[8:11]
    scaled_out, d_both_out, hidden_out, q_out, grad_out = refs[11:16]
    x, table, w, scaled, d_both, hidden, act, slope, q_rows, grad = refs[16:26]
    sem_in, sem_out = refs[26:]
    y, z_lo, core, z_hi = sc[0], sc[1], sc[2], sc[3]
    tile = ROWS // 2
    loads, stores = [], []

    def fetch(src, dst):
        copy = pltpu.make_async_copy(src, dst, sem_in.at[len(loads)])
        copy.start()
        loads.append(copy)
        return copy

    def put(src, dst):
        copy = pltpu.make_async_copy(src, dst, sem_out.at[len(stores)])
        copy.start()
        stores.append(copy)

    own = pl.multiple_of(z_hi * 1024, 1024)
    oth = pl.multiple_of((1 - z_hi) * 1024, 1024)
    w_copies = [
        fetch(w_own, w.at[pl.ds(own, 1024)]),
        fetch(w_oth, w.at[pl.ds(oth, 1024)]),
    ]
    fetch_x = lambda m: fetch(
        x_in.at[pl.ds(m * tile, tile)], x.at[pl.ds(m * tile, tile)]
    )
    x_copies = [fetch_x(0)]
    lane = lax.broadcasted_iota(jnp.int32, (tile, 128), 1)
    expert = ((y * 2 + z_lo) * 2 + core) * 2 + z_hi

    for m in range(2):
        part = slice(m * tile, (m + 1) * tile)
        if m == 0:
            w_copies[0].wait()
            w_copies[1].wait()
            x_copies.append(fetch_x(1))
            c_copies = [
                fetch(arrived[j], table.at[pl.ds(j * BLK, BLK)]) for j in range(8)
            ]
        x_copies[m].wait()
        both = mm(x[part, :], w[:, : 2 * F])
        gate, up = both[:, :F], both[:, F:]
        logistic = jax.nn.sigmoid(gate)
        activated = gate * logistic
        hidden[part, :] = (activated * up).astype(BF)
        act[part, :] = activated
        slope[part, :] = up * logistic * (1.0 + gate * (1.0 - logistic))
    put(hidden, hidden_out)

    row = lax.broadcasted_iota(jnp.int32, (4 * BLK, 4 * BLK), 0)
    col = lax.broadcasted_iota(jnp.int32, (4 * BLK, 4 * BLK), 1)

    def split(v, size):
        major = sum([(v >= size * n).astype(jnp.int32) for n in range(1, 4)])
        return major, v - size * major

    row_z, row_rest = split(row, BLK)
    row_y, row_s = split(row_rest, CAP)
    col_d, col_rest = split(col, BLK)
    col_z, col_s = split(col_rest, CAP)
    turn = (
        (row_z == col_z) & (row_s == col_s) & (row_y == ((y - col_d) & 3))
    ).astype(F32).astype(BF)
    for copy in c_copies:
        copy.wait()
    for dc in range(2):
        from_core = core ^ dc
        for n in range(0, D, 512):
            moved = mm(turn, table[dc * 4 * BLK : (dc + 1) * 4 * BLK, n : n + 512]).astype(BF)
            for z in range(4):
                place = (z % 2) * 4 + from_core * 2 + z // 2
                start = pl.multiple_of(place * BLK, 16)
                scaled[pl.ds(start, BLK), n : n + 512] = moved[z * BLK : (z + 1) * BLK, :]
    put(scaled, scaled_out)

    for m in range(2):
        part = slice(m * tile, (m + 1) * tile)
        total = mm(scaled[part, :], w[:, 2 * F : 3 * F])
        d_both[part, :] = jnp.concatenate(
            [(total * slope[part, :]).astype(BF), (total * act[part, :]).astype(BF)], axis=1
        )
        q = jnp.sum(total * hidden[part, :].astype(F32), axis=1, keepdims=True)
        q_rows[part, :] = jnp.where(lane == expert, q, 0.0).astype(BF)
    put(d_both, d_both_out)
    put(q_rows, q_out)

    for i in range(4):
        start = pl.multiple_of(oth + i * 256, 256)
        line = slice(i * 256, (i + 1) * 256)
        grad[line, : 2 * F] = mm(x[:, pl.ds(start, 256)], d_both[...], 0, 0).astype(BF)
        grad[line, 2 * F : 3 * F] = mm(scaled[:, pl.ds(start, 256)], hidden[...], 0, 0).astype(BF)
        grad[line, 3 * F :] = jnp.zeros((256, PACK - 3 * F), BF)
        put(grad.at[pl.ds(i * 256, 256)], grad_out.at[pl.ds(i * 256, 256)])
    for copy in stores:
        copy.wait()


def expert_pass(sc, x_rows, arrived, w_own, w_oth):
    anywhere = pl.BlockSpec(memory_space=pl.ANY)
    shapes = [(ROWS, D), (ROWS, 2 * F), (ROWS, F), (ROWS, 128), (1024, PACK)]
    scratch = [
        ((ROWS, D), BF),
        ((ROWS, D), BF),
        ((D, PACK), BF),
        ((ROWS, D), BF),
        ((ROWS, 2 * F), BF),
        ((ROWS, F), BF),
        ((ROWS, F), F32),
        ((ROWS, F), F32),
        ((ROWS, 128), BF),
        ((1024, PACK), BF),
    ]
    return pl.pallas_call(
        expert_kernel,
        in_specs=[pl.BlockSpec(memory_space=pltpu.SMEM)] + [anywhere] * 11,
        out_specs=[anywhere] * 5,
        out_shape=[jax.ShapeDtypeStruct(shape, BF) for shape in shapes],
        scratch_shapes=[pltpu.VMEM(*item) for item in scratch]
        + [pltpu.SemaphoreType.DMA((12,)), pltpu.SemaphoreType.DMA((8,))],
        compiler_params=params(),
        cost_estimate=cost(2 * ROWS * D * 6 * F, 32 * MIB),
    )(sc, *arrived, x_rows, w_own, w_oth)


def inputs_kernel(sc, d_both_in, q, w_own, w_oth, dx_out, d_both, w, dx, sem_in, sem_out):
    z_hi = sc[3]
    tile = ROWS // 2
    own = pl.multiple_of(z_hi * 1024, 1024)
    oth = pl.multiple_of((1 - z_hi) * 1024, 1024)
    pairs = (
        (d_both_in, d_both),
        (w_own.at[:, pl.ds(0, 2 * F)], w.at[0]),
        (w_oth.at[:, pl.ds(0, 2 * F)], w.at[1]),
    )
    loads = [pltpu.make_async_copy(*pair, sem_in.at[i]) for i, pair in enumerate(pairs)]
    stores = []
    for copy in loads:
        copy.start()
    extra = q[...].astype(F32)
    loads[0].wait()
    for side, start in enumerate((own, oth)):
        loads[1 + side].wait()
        for m in range(2):
            part = slice(m * tile, (m + 1) * tile)
            rows = mm(d_both[part, :], w[side], 1, 1)
            for to_y in range(4):
                for j in range(4):
                    first, block = j * BLK + to_y * CAP, to_y * 8 + m * 4 + j
                    dx[block, :, pl.ds(start, 1024)] = rows[first : first + CAP, :].astype(BF)
                    if side:
                        first += m * tile
                        dx[block, :, D:] = extra[first : first + CAP, :].astype(BF)
                if side:
                    span = pl.ds(to_y * 8 + m * 4, 4)
                    copy = pltpu.make_async_copy(
                        dx.at[span], dx_out.at[span], sem_out.at[len(stores)]
                    )
                    copy.start()
                    stores.append(copy)
    for copy in stores:
        copy.wait()


def input_grads(sc, d_both, q, w_own, w_oth):
    anywhere = pl.BlockSpec(memory_space=pl.ANY)
    scratch = [(ROWS, 2 * F), (2, 1024, 2 * F), (EXPERTS, CAP, WIDE)]
    return pl.pallas_call(
        inputs_kernel,
        in_specs=[
            pl.BlockSpec(memory_space=pltpu.SMEM),
            anywhere,
            pl.BlockSpec(memory_space=pltpu.VMEM),
            anywhere,
            anywhere,
        ],
        out_specs=anywhere,
        out_shape=jax.ShapeDtypeStruct((EXPERTS, CAP, WIDE), BF),
        scratch_shapes=[pltpu.VMEM(shape, BF) for shape in scratch]
        + [pltpu.SemaphoreType.DMA((3,)), pltpu.SemaphoreType.DMA((8,))],
        compiler_params=params(),
        cost_estimate=cost(2 * ROWS * D * 2 * F, 16 * MIB),
    )(sc, d_both, q, w_own, w_oth)


def grads_kernel(sc, x_in, scaled_in, d_both_in, hidden_in, grad_out, *refs):
    x, scaled, d_both, hidden, grad, sem_in, sem_out = refs
    own = pl.multiple_of(sc[3] * 1024, 1024)
    pairs = (
        (d_both_in, d_both),
        (x_in.at[:, pl.ds(own, 1024)], x),
        (hidden_in, hidden),
        (scaled_in.at[:, pl.ds(own, 1024)], scaled),
    )
    loads = [pltpu.make_async_copy(*pair, sem_in.at[i]) for i, pair in enumerate(pairs)]
    stores = []
    for copy in loads:
        copy.start()
    for copy in loads:
        copy.wait()
    for i in range(4):
        line = slice(i * 256, (i + 1) * 256)
        grad[line, : 2 * F] = mm(x[:, line], d_both[...], 0, 0).astype(BF)
        grad[line, 2 * F : 3 * F] = mm(scaled[:, line], hidden[...], 0, 0).astype(BF)
        grad[line, 3 * F :] = jnp.zeros((256, PACK - 3 * F), BF)
        span = pl.ds(i * 256, 256)
        copy = pltpu.make_async_copy(grad.at[span], grad_out.at[span], sem_out.at[i])
        copy.start()
        stores.append(copy)
    for copy in stores:
        copy.wait()


def own_grads(sc, x_rows, scaled, d_both, hidden):
    anywhere = pl.BlockSpec(memory_space=pl.ANY)
    scratch = [(ROWS, 1024), (ROWS, 1024), (ROWS, 2 * F), (ROWS, F), (1024, PACK)]
    return pl.pallas_call(
        grads_kernel,
        in_specs=[pl.BlockSpec(memory_space=pltpu.SMEM)] + [anywhere] * 4,
        out_specs=anywhere,
        out_shape=jax.ShapeDtypeStruct((1024, PACK), BF),
        scratch_shapes=[pltpu.VMEM(shape, BF) for shape in scratch]
        + [pltpu.SemaphoreType.DMA((4,)), pltpu.SemaphoreType.DMA((4,))],
        compiler_params=params(),
        cost_estimate=cost(2 * ROWS * 1024 * 3 * F, 12 * MIB),
    )(sc, x_rows, scaled, d_both, hidden)


def hold_kernel(value, *rest):
    pass


def hold(value, *after):
    anywhere = pl.BlockSpec(memory_space=pl.ANY)
    return pl.pallas_call(
        hold_kernel,
        in_specs=[anywhere] * (1 + len(after)),
        out_specs=anywhere,
        out_shape=jax.ShapeDtypeStruct(value.shape, value.dtype),
        input_output_aliases={0: 0},
        compiler_params=params(),
    )(value, *after)


def final_kernel(back, routes, probs, out, out_probs, sel, rows):
    experts = lax.broadcasted_iota(jnp.int32, (EXPERTS, TOK), 0)
    mask = jnp.zeros((EXPERTS, TOK), F32)
    for k in range(TOP):
        mask = jnp.where(routes[k : k + 1, :] == experts, 1.0, mask)
    earlier = (
        lax.broadcasted_iota(jnp.int32, (TOK, TOK), 0)
        < lax.broadcasted_iota(jnp.int32, (TOK, TOK), 1)
    ).astype(BF)
    place = jnp.where(mask > 0.5, mm(mask.astype(BF), earlier), -1.0)
    slot = lax.broadcasted_iota(jnp.int32, (SLOT, TOK), 0).astype(F32)
    for e in range(EXPERTS):
        line = slice(e * SLOT, (e + 1) * SLOT)
        sel[line, :] = (slot == place[e : e + 1, :]).astype(F32).astype(BF)
        rows[e, :CAP, :] = back[e]
        rows[e, CAP:, :] = jnp.zeros((SLOT - CAP, WIDE), BF)
    table = rows[...].reshape(EXPERTS * SLOT, WIDE)
    for n in range(0, D, 512):
        out[:, n : n + 512] = mm(sel[...], table[:, n : n + 512], 0, 0).astype(BF)
    values = mm(table[:, D:], sel[...], 0, 0)
    weight = probs[...].astype(BF).astype(F32)
    line = lax.broadcasted_iota(jnp.int32, (128, TOK), 0)
    for k in range(TOP):
        value = jnp.sum(
            jnp.where(line == routes[k : k + 1, :], values, 0.0), axis=0, keepdims=True
        )
        out_probs[k : k + 1, :] = value / weight[k : k + 1, :]


def final(back, routes, probs):
    return pl.pallas_call(
        final_kernel,
        out_shape=[
            jax.ShapeDtypeStruct((TOK, D), BF),
            jax.ShapeDtypeStruct((TOP, TOK), F32),
        ],
        scratch_shapes=[
            pltpu.VMEM((EXPERTS * SLOT, TOK), BF),
            pltpu.VMEM((EXPERTS, SLOT, WIDE), BF),
        ],
        compiler_params=params(),
        cost_estimate=cost(FINAL_FLOPS, 8 * MIB),
    )(back, routes, probs)


def place_kernel(sc, own, oth, gate_up, down, turned, sems):
    copies = []
    for i, (part, which) in enumerate(((oth, 1 - sc[3]), (own, sc[3]))):
        copy = pltpu.make_async_copy(
            part.at[:, pl.ds(0, 2 * F)], gate_up.at[which], sems.at[2 * i]
        )
        copy.start()
        turned[i] = part[:, 2 * F : 3 * F].T
        after = pltpu.make_async_copy(turned.at[i], down.at[which], sems.at[2 * i + 1])
        after.start()
        copies += [copy, after]
    for copy in copies:
        copy.wait()


def place(sc, own, oth):
    vmem = pl.BlockSpec(memory_space=pltpu.VMEM)
    return pl.pallas_call(
        place_kernel,
        in_specs=[pl.BlockSpec(memory_space=pltpu.SMEM), vmem, vmem],
        out_specs=[pl.BlockSpec(memory_space=pl.ANY)] * 2,
        out_shape=[
            jax.ShapeDtypeStruct((2, 256, 2 * F), BF),
            jax.ShapeDtypeStruct((2, F, 256), BF),
        ],
        scratch_shapes=[pltpu.VMEM((2, F, 256), BF), pltpu.SemaphoreType.DMA((4,))],
        compiler_params=params(),
        cost_estimate=cost(0, 5 * MIB),
    )(sc, own, oth)


def z_index(z):
    return (z % 2) * 2 + z // 2


def along_y(k):
    return [(y, (y + k) % 4) for y in range(4)]


def along_z(k):
    return [(z_index(z), z_index((z + k) % 4)) for z in range(4)]


def along_yc(k, dc):
    return [(y * 2 + c, ((y + k) % 4) * 2 + (c ^ dc)) for y in range(4) for c in range(2)]


def body(tokens, cotangent, routes, probs, w_gate_up, w_down):
    names = ("y", "zl", "c", "zh", "x")
    sc = jnp.stack([lax.axis_index(n) for n in names]).astype(jnp.int32)
    tok, cot, own, oth = prepare(
        sc, tokens, cotangent, routes.T, probs.T, w_gate_up, w_down
    )
    cots = [cot] + [lax.ppermute(cot, ("zl", "zh"), along_z(k)) for k in (1, 2, 3)]
    toks = lax.all_to_all(tok, "y", split_axis=0, concat_axis=0, tiled=True)
    swap = [(0, 1), (1, 0)]
    gather = lambda w: lax.all_gather(w, "x", axis=0, tiled=True)
    oth = hold(lax.ppermute(oth, "zh", swap), toks, *cots[1:])
    x_send, sent = pick(sc, toks, cots)
    w_own, w_oth = gather(own), gather(oth)

    x_rows = lax.all_to_all(
        x_send.reshape(8, BLK, D), ("zl", "c", "zh"), split_axis=0, concat_axis=0, tiled=True
    ).reshape(ROWS, D)
    arrived = [
        sent[j] if j == 0 else lax.ppermute(sent[j], ("y", "c"), along_yc(j % 4, j // 4))
        for j in range(8)
    ]
    scaled, d_both, hidden, q, oth_part = expert_pass(sc, x_rows, arrived, w_own, w_oth)

    scatter = lambda g: lax.psum_scatter(g, "x", scatter_dimension=0, tiled=True)
    oth_sum = lax.ppermute(scatter(oth_part), "zh", swap)
    dx = input_grads(sc, d_both, q, w_own, w_oth)
    own_sum = scatter(own_grads(sc, x_rows, scaled, d_both, hidden))
    back = lax.all_to_all(
        dx, ("y", "zl", "c", "zh"), split_axis=0, concat_axis=0, tiled=True
    )
    d_tokens, d_probs = final(back, routes.T, probs.T)
    grad_gu, grad_dn = place(sc, own_sum, oth_sum)
    return d_tokens, d_probs.T, grad_gu, grad_dn


def solution(mesh):
    fine = Mesh(mesh.devices.reshape(4, 2, 2, 2, 4), ("y", "zl", "c", "zh", "x"))
    exp, fsdp = ("y", "zl", "c"), ("zh", "x")
    row = P(exp + fsdp, None)
    gate_up, down = P(exp, fsdp, None), P(exp, None, fsdp)
    return jax.shard_map(
        body,
        mesh=fine,
        in_specs=(row, row, row, row, gate_up, down),
        out_specs=(row, row, gate_up, down),
        check_vma=False,
    )
```
